128 devices in a mesh: gx: 8 (over y, core), gy: 16 (over x, z).
Axes of the slice: x: 4, y: 4, z: 4, core: 2. Of those that a mesh axis runs over, the one named last changes fastest.
Arguments:
- positions: float32 [3, 2097152], P(None, ('gx', 'gy')), may hold values from 0 to 4
- charges: float32 [2097152], P(('gx', 'gy')), may hold values from -6 to 6
- counts: int32 [16384], P(('gx', 'gy')), may hold values from 1 to 128
- centres: float32 [3, 16384], P(None, ('gx', 'gy')), may hold values from 0 to 4
- freqs: float32 [3, 256], replicated, may hold values from -4 to 4
- phases: float32 [256], replicated, may hold values from -3.140625 to 3.140625
- m2m: bfloat16 [8, 256, 256], replicated, may hold values from -0.125 to 0.125
- m2l: bfloat16 [64, 256, 256], replicated, may hold values from -0.02734375 to 0.02734375
- send_nodes: int32 [128, 16, 32], P(('gx', 'gy')), may hold values from 0 to 143
- v_source: int32 [16384, 189], P(('gx', 'gy')), may hold values from 0 to 655
- v_offset: int32 [16384, 189], P(('gx', 'gy')), may hold values from 0 to 63
- u_source: int32 [16384, 27], P(('gx', 'gy')), may hold values from 0 to 383
Outputs:
- potential: float32 [2097152], P(('gx', 'gy'))
The draws below stay inside these ranges and needn't reach their ends.
All inputs are finite; a program needn't handle non-finite values.
Results may differ from the reference program's by a relative error of at most 0.0027.
Values may be sent and summed in bfloat16 or wider, within the bound.
No kernel may reach another device: no remote copies, remote signals or barrier semaphores. Data moves between devices by JAX's collectives and lax.ppermute only.
A program may use at most 128 MiB of HBM per device.

```python
import jax
import jax.numpy as jnp
from jax import lax

MP = 256
LEAF_SIZE = 128
OFFSETS = 64
VLIST = 189
ULIST = 27
LEAF_DEV = 128
REACH = 8
HALO = 128
NODES_DEV = 144
CAP = 32
SHIFTS = 16
LEAVES = 16384
PARTICLES = 2097152
TABLE = 656
N_GX = 8
N_GY = 16
DEVICES = 128


def with_ends(values, key, smallest, high):
    longest = values.shape.index(max(values.shape))
    spots = []
    for shift in (0, 1):
        where = [jax.random.randint(jax.random.fold_in(key, axis), (), 0, length) for axis, length in enumerate(values.shape)]
        where[longest] = (where[longest] + shift) % values.shape[longest]
        spots.append(tuple(where))
    return values.at[spots[0]].set(smallest).at[spots[1]].set(high)


def steps_of(stream_key, extent, shards, smallest, top_value):
    loudness, own = 1.0, jax.random.fold_in(stream_key, 6)
    for dim, shards_of in shards:
        draws = jnp.exp(jax.random.uniform(jax.random.fold_in(own, dim), (shards_of,), jnp.float32, smallest / len(shards), top_value / len(shards)))
        loudness = loudness * jnp.repeat(draws, extent[dim] // shards_of).reshape([-1 if axis == dim else 1 for axis in range(len(extent))])
    return loudness


def gaussian(key, dims, spread, limit, pieces=(), held_as=jnp.bfloat16):
    entries = spread * jax.random.normal(key, dims, jnp.float32)
    if pieces:
        entries = entries * steps_of(key, dims, pieces, -0.22, 0.18)
    return jnp.clip(entries, -limit, limit).astype(held_as)


def setup_inputs(seed: int = 0) -> dict:
    key_list = jax.random.split(jax.random.key(seed), 13)
    positions = jnp.clip(4.0 * jax.random.uniform(key_list[0], (3, PARTICLES), jnp.float32) ** steps_of(key_list[0], (3, PARTICLES), ((1, 128),), -0.2, 0.2), 0.0, 4.0)
    charges = gaussian(key_list[1], (PARTICLES,), 1.0, 6.0, ((0, 128),), jnp.float32)
    counts = with_ends(jax.random.randint(key_list[2], (LEAVES,), 1, LEAF_SIZE + 1), jax.random.fold_in(key_list[2], 1), 1, LEAF_SIZE).astype(jnp.int32)
    centres = jnp.clip(4.0 * jax.random.uniform(key_list[3], (3, LEAVES), jnp.float32) ** steps_of(key_list[3], (3, LEAVES), ((1, 128),), -0.2, 0.2), 0.0, 4.0)
    freqs = gaussian(key_list[4], (3, MP), 1.0, 4.0, (), jnp.float32)
    phases = jnp.clip(jax.random.uniform(key_list[5], (MP,), jnp.float32, -3.140625, 3.140625), -3.140625, 3.140625)
    m2m = gaussian(key_list[6], (8, MP, MP), (8 * MP) ** -0.5, 0.125)
    m2l = gaussian(key_list[7], (OFFSETS, MP, MP), (VLIST * MP) ** -0.5, 0.02734375)
    send_nodes = with_ends(jax.random.randint(key_list[8], (DEVICES, SHIFTS, CAP), 0, NODES_DEV), jax.random.fold_in(key_list[8], 1), 0, NODES_DEV - 1).astype(jnp.int32)
    v_source = with_ends(jax.random.randint(key_list[9], (LEAVES, VLIST), 0, TABLE), jax.random.fold_in(key_list[9], 1), 0, TABLE - 1).astype(jnp.int32)
    v_offset = with_ends(jax.random.randint(key_list[10], (LEAVES, VLIST), 0, OFFSETS), jax.random.fold_in(key_list[10], 1), 0, OFFSETS - 1).astype(jnp.int32)
    u_source = with_ends(jax.random.randint(key_list[11], (LEAVES, ULIST), 0, LEAF_DEV + 2 * HALO), jax.random.fold_in(key_list[11], 1), 0, (LEAF_DEV + 2 * HALO) - 1).astype(jnp.int32)
    return dict(positions=positions, charges=charges, counts=counts, centres=centres, freqs=freqs, phases=phases, m2m=m2m, m2l=m2l, send_nodes=send_nodes, v_source=v_source, v_offset=v_offset, u_source=u_source)


def basis_of(rel, freqs, phases):
    angle = jnp.einsum('cln,ck->lnk', rel, freqs, precision=lax.Precision.HIGHEST) + phases
    return jnp.cos(angle)

def near_field(spots, widened, u_list):
    leaves = spots.shape[1]
    groups = leaves // 8
    slot_ids = jnp.arange(LEAF_SIZE)

    def group_fn(args):
        here, lists, leaf_ids = args
        source = widened[:, lists]
        diff = here[:, :, :, None, None] - source[:3, :, None, :, :]
        dist2 = lax.optimization_barrier(jnp.sum(diff * diff, axis=0))
        own = lists[:, None, :, None] == (HALO + leaf_ids)[:, None, None, None]
        same = slot_ids[None, :, None, None] == slot_ids[None, None, None, :]
        term = source[3][:, None, :, :] / jnp.sqrt(dist2 + 0.01)
        term = jnp.where(own & same, jnp.float32(0.0), term)
        return lax.optimization_barrier(jnp.sum(term, axis=(2, 3))) * (ULIST * LEAF_SIZE) ** (-0.5)
    here_g = spots.reshape(3, groups, 8, LEAF_SIZE).transpose(1, 0, 2, 3)
    lists_g = u_list.reshape(groups, 8, ULIST)
    ids_g = jnp.arange(leaves, dtype=jnp.int32).reshape(groups, 8)
    out = lax.map(group_fn, (here_g, lists_g, ids_g))
    return out.reshape(leaves, LEAF_SIZE)

def reference(positions, charges, counts, centres, freqs, phases, m2m, m2l, send_nodes, v_source, v_offset, u_source):
    ndev = N_GX * N_GY
    live = (jnp.arange(LEAF_SIZE, dtype=jnp.int32)[None, :] < counts[:, None]).astype(jnp.float32)
    charge = charges.reshape(LEAVES, LEAF_SIZE) * live
    spots_all = positions.reshape(3, LEAVES, LEAF_SIZE)
    spots_dev = spots_all.reshape(3, ndev, LEAF_DEV, LEAF_SIZE).transpose(1, 0, 2, 3)
    charge_dev = charge.reshape(ndev, LEAF_DEV, LEAF_SIZE)
    live_dev = live.reshape(ndev, LEAF_DEV, LEAF_SIZE)
    centre_dev = centres.reshape(3, ndev, LEAF_DEV).transpose(1, 0, 2)

    def upward(args):
        spots, charge_d, centre = args
        basis = basis_of(spots - centre[:, :, None], freqs, phases)
        leaf_mult = (jnp.einsum('ln,lnk->lk', charge_d, basis, precision=lax.Precision.HIGHEST) * LEAF_SIZE ** (-0.5)).astype(jnp.bfloat16)
        parent = jnp.einsum('pck,ckj->pj', leaf_mult.reshape(LEAF_DEV // 8, 8, MP).astype(jnp.float32), m2m.astype(jnp.float32)).astype(jnp.bfloat16)
        return jnp.concatenate([leaf_mult, parent], axis=0)
    nodes = lax.map(upward, (spots_dev, charge_dev, centre_dev))
    widened_all = jnp.concatenate([spots_all, charge[None]], axis=0)
    padded = jnp.pad(widened_all, ((0, 0), (HALO, HALO), (0, 0)))
    shift_ids = jnp.arange(SHIFTS, dtype=jnp.int32)
    distance = jnp.where(shift_ids < REACH, shift_ids + 1, REACH - 1 - shift_ids).astype(jnp.int32)

    def target(args):
        dev, spots, charge_d, centre, live_d, vs, vo, us = args
        anchor = dev - distance
        valid = (anchor >= 0) & (anchor < ndev)
        safe = jnp.clip(anchor, 0, ndev - 1).astype(jnp.int32)
        rows = send_nodes[safe, shift_ids]
        ghosts = nodes[safe[:, None], rows]
        ghosts = jnp.where(valid[:, None, None], ghosts, jnp.zeros_like(ghosts))
        table = jnp.concatenate([nodes[dev], ghosts.reshape(SHIFTS * CAP, MP)], axis=0)
        gathered = table[vs].astype(jnp.float32)
        onehot = (vo[:, :, None] == jnp.arange(OFFSETS, dtype=jnp.int32)[None, None, :]).astype(jnp.float32)
        summed = jnp.einsum('lvo,lvk->lok', onehot, gathered).astype(jnp.bfloat16)
        local = jnp.dot(summed.reshape(LEAF_DEV, OFFSETS * MP), m2l.reshape(OFFSETS * MP, MP), preferred_element_type=jnp.float32)
        basis = basis_of(spots - centre[:, :, None], freqs, phases)
        far = jnp.einsum('lnk,lk->ln', basis, local, precision=lax.Precision.HIGHEST) * MP ** (-0.5)
        widened = lax.dynamic_slice_in_dim(padded, (dev * LEAF_DEV).astype(jnp.int32), LEAF_DEV + 2 * HALO, axis=1)
        near = near_field(spots, widened, us)
        return (far + near) * live_d
    out = lax.map(target, (jnp.arange(ndev, dtype=jnp.int32), spots_dev, charge_dev, centre_dev, live_dev, v_source.reshape(ndev, LEAF_DEV, VLIST), v_offset.reshape(ndev, LEAF_DEV, VLIST), u_source.reshape(ndev, LEAF_DEV, ULIST)))
    return out.reshape(PARTICLES)
```

```python
import math

import jax
import jax.numpy as jnp
import numpy as np
from jax import lax
from jax.experimental import pallas as pl
from jax.experimental.pallas import tpu as pltpu
from jax.sharding import PartitionSpec as P

F32 = jnp.float32
BF = jnp.bfloat16
MP = 256
LEAF = 128
OFFSETS = 64
VLIST = 189
ULIST = 27
CAP = 32
REACH = 8
SHIFTS = 16
AXES = ("gx", "gy")
ROWS = 256
MIB = 2**20
SM = pl.BlockSpec(memory_space=pltpu.SMEM)
VM = pl.BlockSpec(memory_space=pltpu.VMEM)
HBM = pl.BlockSpec(memory_space=pl.ANY)
NT = (((1,), (1,)), ((), ()))


def sine_coefficients(terms=4):
    f = 0.5 * np.cos(np.pi * (np.arange(400) + 0.5) / 800)
    target = math.sqrt(2.0) * np.sin(np.pi * f)
    basis = np.stack([f ** (2 * k + 1) for k in range(terms)], axis=1)
    return [float(c) for c in np.linalg.lstsq(basis, target, rcond=None)[0]]


SINE = sine_coefficients()


def rounded(v):
    return v.astype(BF).astype(F32)


def split3(v):
    a = rounded(v)
    b = rounded(v - a)
    return a, b, v - a - b


def pick3(rows, x, y, z):
    m = rows % 3
    return jnp.where(m == 0, x, jnp.where(m == 1, y, z))


def dot(a, b):
    return jnp.dot(a, b, preferred_element_type=F32)


def dense_rows(count):
    return (count + 7) & -8


def row_ranges(counts_row):
    leaves = counts_row.shape[1]
    sub = lax.broadcasted_iota(jnp.int32, (leaves, leaves), 0)
    lane = lax.broadcasted_iota(jnp.int32, (leaves, leaves), 1)
    size = jnp.broadcast_to(dense_rows(counts_row), (leaves, leaves)).astype(F32)
    first = jnp.sum(jnp.where(lane < sub, size, 0.0), axis=1, keepdims=True)
    last = jnp.sum(jnp.where(lane <= sub, size, 0.0), axis=1, keepdims=True)
    return first.astype(jnp.int32), last.astype(jnp.int32)


def up_kernel(
    counts_ref, centres_ref, high_ref, stacked_ref, counts_row_ref, freqs_ref, phases_ref, m2m_ref, send_ref,
    basis_ref, nodes_ref, out_ref, sel_ref, dense, total, mult,
):
    leaves = counts_row_ref.shape[1]
    rows = lax.broadcasted_iota(jnp.int32, (32, LEAF), 0)

    def pack(l, off):
        part = [jnp.broadcast_to(stacked_ref[pl.ds(c * leaves + l, 1), :], (32, LEAF)) for c in range(4)]
        rel = pick3(rows, *[part[c] - centres_ref[c * leaves + l] for c in range(3)])
        a, b, c = split3(rel)
        full = jnp.where(
            rows < 9, a,
            jnp.where(rows < 15, b, jnp.where(rows < 18, c, jnp.where(rows < 21, 1.0, jnp.where(rows == 24, part[3], 0.0)))),
        )
        dense[pl.ds(pl.multiple_of(off, 8), LEAF), :] = full.T
        return off + dense_rows(counts_ref[l])

    def pack4(i, off):
        for k in range(4):
            off = pack(i * 4 + k, off)
        return off

    used = lax.fori_loop(0, leaves // 4, pack4, jnp.int32(0))
    dense[pl.ds(pl.multiple_of(used, 8), ROWS), :] = jnp.zeros((ROWS, 32), F32)

    wide_rows = lax.broadcasted_iota(jnp.int32, (32, MP), 0)
    turn = pick3(wide_rows, *[jnp.broadcast_to(freqs_ref[c:c + 1, :], (32, MP)) for c in range(3)])
    turn = jnp.where(wide_rows < 18, turn, jnp.broadcast_to(phases_ref[...], (32, MP))) * (0.5 / math.pi)
    a, b, c = split3(turn)
    g = wide_rows // 3
    weights = jnp.where(
        wide_rows < 18,
        jnp.where((g == 0) | (g == 3) | (g == 5), a, jnp.where((g == 1) | (g == 4), b, c)),
        jnp.where(wide_rows == 18, a, jnp.where(wide_rows == 19, b, jnp.where(wide_rows == 20, c, 0.0))),
    ).astype(BF)

    first, last = row_ranges(counts_row_ref[...])
    lane = lax.broadcasted_iota(jnp.int32, (leaves, ROWS), 1)
    total[...] = jnp.zeros_like(total)

    def step(i, _):
        base = pl.multiple_of(i * ROWS, ROWS)
        rel = dense[pl.ds(base, ROWS), :]
        turns = dot(rel.astype(BF), weights)
        f = turns - jnp.round(turns)
        u = f * f
        s = SINE[3]
        for k in (2, 1, 0):
            s = s * u + SINE[k]
        s = s * f
        basis = 1.0 - s * s
        basis_ref[pl.ds(base, ROWS), :] = basis.astype(BF)
        w = basis * rel[:, 24:25]
        hi = w.astype(BF)
        lo = (w - hi.astype(F32)).astype(BF)
        member = ((lane >= first - base) & (lane < last - base)).astype(F32).astype(BF)
        total[...] += dot(member, hi) + dot(member, lo)
        return 0

    lax.fori_loop(0, (used + ROWS - 1) // ROWS, step, 0)
    leaf_mult = (total[...] * LEAF ** (-0.5)).astype(BF)
    for h in range(2):
        mult[h, :, :] = leaf_mult[:, h * LEAF:(h + 1) * LEAF].astype(F32)
    parents = leaves // 8
    parent = jnp.zeros((parents, MP), F32)
    for c in range(8):
        child = jnp.concatenate([mult[h, pl.ds(c, parents, stride=8), :] for h in range(2)], axis=1)
        parent += dot(child.astype(BF), m2m_ref[c])
    nodes_ref[0:leaves, :] = leaf_mult
    nodes_ref[leaves:leaves + parents, :] = parent.astype(BF)
    ids = lax.broadcasted_iota(jnp.int32, (SHIFTS * CAP, leaves + parents), 1)
    chosen = (send_ref[...] == ids).astype(F32).astype(BF)
    out_ref[...] = dot(chosen, nodes_ref[...]).astype(BF)
    half = REACH * CAP
    sel_ref[...] = out_ref[pl.ds(pl.multiple_of((1 - high_ref[0]) * half, half), half), :]


def slots_kernel(gy_ref, out_ref, recv_ref, slots_ref):
    gy = gy_ref[0]
    for t in range(SHIFTS):
        for sub in range(2):
            ahead = (t - gy) if sub == 0 else (gy - t)
            b = (ahead & (SHIFTS - 1)) - 1
            valid = (b >= 0) & (b < REACH)
            b = jnp.clip(b, 0, REACH - 1)
            own = out_ref[pl.ds(pl.multiple_of((sub * REACH + b) * CAP, CAP), CAP), :]
            far = recv_ref[pl.ds(pl.multiple_of(b * CAP, CAP), CAP), :]
            value = jnp.where(ahead > 0, own, far)
            slots_ref[pl.ds((2 * t + sub) * CAP, CAP), :] = jnp.where(valid, value, jnp.zeros_like(value))


NEAR_BIG, NEAR_SMALL = 64, 32


def near_kernel(
    counts_ref, us_ref, prev_ref, own_ref, next_ref, usv_ref,
    near_ref, feat, charge, tgt, acc_ref, big, small,
):
    leaves = near_ref.shape[0]
    rows = lax.broadcasted_iota(jnp.int32, (8, LEAF), 0)

    def coords(ref, l):
        return [jnp.broadcast_to(ref[pl.ds(c * leaves + l, 1), :] - 2.0, (8, LEAF)) for c in range(3)]

    for part, ref in enumerate((prev_ref, own_ref, next_ref)):

        def build(i, _, part=part, ref=ref):
            for k in range(8):
                l = i * 8 + k
                x, y, z = coords(ref, l)
                n1, n2, n3 = split3(x * x + y * y + z * z)
                s1, s2, s3 = split3(-2.0 * pick3(rows, x, y, z))
                a = jnp.where(rows < 3, s1, jnp.where(rows < 6, s2, jnp.where(rows == 6, n1, n2)))
                b = jnp.where(rows < 3, s3, jnp.where(rows == 3, n3, 1.0))
                s = part * leaves + l
                feat[pl.ds(pl.multiple_of(s * 16, 16), 16), :] = jnp.concatenate([a, b], axis=0).astype(BF)
                charge[pl.ds(pl.multiple_of(s * 8, 8), 8), :] = jnp.broadcast_to(
                    ref[pl.ds(3 * leaves + l, 1), :], (8, LEAF)
                )
            return 0

        lax.fori_loop(0, leaves // 8, build, 0)

    def targets(i, _):
        for k in range(4):
            l = i * 4 + k
            x, y, z = coords(own_ref, l)
            n1, n2, n3 = split3(x * x + y * y + z * z + 0.01)
            s1, s2, s3 = split3(pick3(rows, x, y, z))
            zero = jnp.zeros_like(x)
            a1 = jnp.where(rows < 6, s1, 1.0)
            tail = jnp.where(rows == 5, n1, jnp.where(rows == 6, n2, n3))
            b1 = jnp.where(rows < 3, s1, jnp.where(rows == 3, 1.0, jnp.where(rows == 4, 0.0, tail)))
            a2 = jnp.where(rows < 6, s2, 0.0)
            a3 = jnp.where(rows < 3, s3, 0.0)
            full = jnp.concatenate([a1, b1, a2, zero, a3, zero], axis=0)
            tgt[pl.ds(pl.multiple_of(l * LEAF, LEAF), LEAF), :] = full.T.astype(BF)
        return 0

    lax.fori_loop(0, leaves // 4, targets, 0)

    def listing(l, state):
        n, m = state
        count = counts_ref[l]
        for c in range(LEAF // NEAR_BIG):
            left = count - c * NEAR_BIG
            place = l * LEAF + c * NEAR_BIG
            big[n] = place
            n = n + (left > NEAR_SMALL).astype(jnp.int32)
            small[m] = place
            m = m + ((left > 0) & (left <= NEAR_SMALL)).astype(jnp.int32)
        return n, m

    n_big, n_small = lax.fori_loop(0, leaves, listing, (jnp.int32(0), jnp.int32(0)))

    def run(items, n, size, unroll):
        for k in range(unroll):
            items[n + k] = leaves * LEAF

        def work(i, _):
            for k in range(unroll):
                place = items[i * unroll + k]
                safe = jnp.minimum(place, leaves * LEAF - NEAR_BIG)
                l = safe >> 7
                lhs = tgt[pl.ds(pl.multiple_of(safe, NEAR_SMALL), size), :]
                acc = None
                for u in range(0, ULIST, 2):
                    two = [us_ref[l * ULIST + v] for v in range(u, min(u + 2, ULIST))]
                    f = [feat[pl.ds(pl.multiple_of(s * 16, 16), 16), :] for s in two]
                    f = jnp.concatenate(f, axis=1) if len(f) > 1 else f[0]
                    r = lax.rsqrt(dot(lhs, jnp.concatenate([f, f, f], axis=0)))
                    for j, s in enumerate(two):
                        q = charge[pl.ds(pl.multiple_of(s * 8, 8), 8), :]
                        term = r[:, j * LEAF:(j + 1) * LEAF].reshape(size // 8, 8, LEAF) * q[None]
                        acc = term if acc is None else acc + term
                acc_ref[pl.ds(pl.multiple_of(place, NEAR_SMALL), size), :] = acc.reshape(size, LEAF)
            return 0

        lax.fori_loop(0, (n + unroll - 1) // unroll, work, 0)

    run(big, n_big, NEAR_BIG, 4)
    run(small, n_small, NEAR_SMALL, 4)

    def reduce(i, _):
        parts = []
        for k in range(8):
            l = i * 8 + k
            t = acc_ref[pl.ds(pl.multiple_of(l * LEAF, LEAF), LEAF), :].T
            parts.append(jnp.sum(t, axis=0, keepdims=True))
        near_ref[pl.ds(pl.multiple_of(i * 8, 8), 8), :] = jnp.concatenate(parts, axis=0)
        return 0

    lax.fori_loop(0, leaves // 8, reduce, 0)
    own_id = lax.broadcasted_iota(jnp.int32, usv_ref.shape, 0) + leaves
    times = jnp.sum((usv_ref[...] == own_id).astype(F32), axis=1, keepdims=True)
    itself = own_ref[3 * leaves:4 * leaves, :] * lax.rsqrt(jnp.full((1, LEAF), 0.01, F32))
    near_ref[...] = (near_ref[...] - times * itself) * (ULIST * LEAF) ** (-0.5)


GROUP = 16


def down_kernel(
    counts_ref, gy_ref, counts_row_ref, counts_col_ref, nodes_ref, got_ref, vs_ref, vo_ref, near_ref, m2l_hbm, basis_hbm,
    pot_ref, m2l, basis, table, source, offset, tally, summed, local, far, sems,
):
    leaves = near_ref.shape[0]
    m2l_copy = pltpu.make_async_copy(m2l_hbm, m2l, sems.at[0])
    basis_copy = pltpu.make_async_copy(basis_hbm, basis, sems.at[1])
    m2l_copy.start()
    basis_copy.start()
    gy = gy_ref[0]
    own = nodes_ref.shape[0]
    table[0:own, :] = nodes_ref[...]
    for s in range(SHIFTS):
        by = s + 1 if s < REACH else REACH - 1 - s
        block = 2 * ((gy - by) & (SHIFTS - 1)) + (0 if by > 0 else 1)
        table[own + s * CAP:own + (s + 1) * CAP, :] = got_ref[pl.ds(pl.multiple_of(block * CAP, CAP), CAP), :]
    top = own + SHIFTS * CAP
    table[top:, :] = jnp.zeros((table.shape[0] - top, MP), BF)
    source[...] = jnp.full_like(source, -1)
    source[:, 0:VLIST] = vs_ref[...]
    offset[...] = jnp.full_like(offset, -1)
    offset[:, 0:VLIST] = vo_ref[...]
    sub = lax.broadcasted_iota(jnp.int32, (MP, MP), 0).astype(F32).astype(BF)
    one, zero = jnp.ones((), BF), jnp.zeros((), BF)

    def group(g, _):
        for k in range(GROUP):
            l = g * GROUP + k
            o_row = offset[pl.ds(l, 1), :].astype(F32).astype(BF)
            o_hot = jnp.where(sub[0:OFFSETS] == o_row, one, zero)
            s_row = source[pl.ds(l, 1), :]
            for t in range(3):
                size = min(MP, top - t * MP)
                part = jnp.clip(s_row - t * MP, -1, MP).astype(F32).astype(BF)
                s_hot = jnp.where(sub[0:size] == part, one, zero)
                if size < MP:
                    s_hot = jnp.concatenate([s_hot, jnp.zeros((MP - size, MP), BF)], axis=0)
                tally[k * OFFSETS:(k + 1) * OFFSETS, t * MP:(t + 1) * MP] = lax.dot_general(
                    o_hot, s_hot, NT, preferred_element_type=F32
                ).astype(BF)
        both = dot(tally[...], table[...])
        for h in range(2):
            summed[h, pl.ds(pl.multiple_of(g * GROUP * OFFSETS, GROUP * OFFSETS), GROUP * OFFSETS), :] = both[
                :, h * LEAF:(h + 1) * LEAF
            ]
        return 0

    lax.fori_loop(0, leaves // GROUP, group, 0)
    m2l_copy.wait()
    local[...] = jnp.zeros_like(local)

    def translate(i, _):
        parts = [
            summed[h, pl.ds(i * 4 + k, leaves, stride=OFFSETS), :].astype(BF) for k in range(4) for h in range(2)
        ]
        local[...] += dot(jnp.concatenate(parts, axis=1), m2l[pl.ds(pl.multiple_of(i * 4 * MP, 4 * MP), 4 * MP), :])
        return 0

    lax.fori_loop(0, OFFSETS // 4, translate, 0)
    hi = local[...].astype(BF)
    lo = (local[...] - hi.astype(F32)).astype(BF)
    both = jnp.concatenate([hi, lo], axis=0)
    first, last = row_ranges(counts_row_ref[...])
    used = lax.fori_loop(0, leaves, lambda l, off: off + dense_rows(counts_ref[l]), jnp.int32(0))
    lane = lax.broadcasted_iota(jnp.int32, (leaves, ROWS), 1)
    basis_copy.wait()

    def expand(i, _):
        base = pl.multiple_of(i * ROWS, ROWS)
        p = lax.dot_general(both, basis[pl.ds(base, ROWS), :], NT, preferred_element_type=F32)
        p = p[:leaves] + p[leaves:]
        member = (lane >= first - base) & (lane < last - base)
        value = jnp.sum(jnp.where(member, p, 0.0), axis=0, keepdims=True)
        far[pl.ds(2 * i, 1), :] = value[:, :LEAF]
        far[pl.ds(2 * i + 1, 1), :] = value[:, LEAF:]
        return 0

    lax.fori_loop(0, (used + ROWS - 1) // ROWS, expand, 0)
    lane1 = lax.broadcasted_iota(jnp.int32, (1, LEAF), 1)

    def place(i, off):
        parts = []
        for k in range(8):
            l = i * 8 + k
            row, at = off >> 7, off & (LEAF - 1)
            shift = (LEAF - at) & (LEAF - 1)
            a = pltpu.roll(far[pl.ds(row, 1), :], shift, 1)
            b = pltpu.roll(far[pl.ds(row + 1, 1), :], shift, 1)
            parts.append(jnp.where(lane1 < LEAF - at, a, b))
            off = off + dense_rows(counts_ref[l])
        pot_ref[pl.ds(pl.multiple_of(i * 8, 8), 8), :] = jnp.concatenate(parts, axis=0)
        return off

    lax.fori_loop(0, leaves // 8, place, jnp.int32(0))
    lane = lax.broadcasted_iota(jnp.int32, (leaves, LEAF), 1)
    value = pot_ref[...] * MP ** (-0.5) + near_ref[...]
    pot_ref[...] = jnp.where(lane < counts_col_ref[...], value, 0.0)


def per_device(
    positions, charges, counts, centres, freqs, phases, m2m, m2l, send_nodes, v_source, v_offset, u_source
):
    leaves = counts.shape[0]
    n_gx, n_gy = lax.axis_size("gx"), lax.axis_size("gy")
    devices = n_gx * n_gy
    gy = lax.axis_index("gy").astype(jnp.int32).reshape(1)
    high = (gy >= n_gy // 2).astype(jnp.int32)
    live = jnp.arange(LEAF, dtype=jnp.int32)[None, :] < counts[:, None]
    charge = jnp.where(live, charges.reshape(leaves, LEAF), 0.0)
    stacked = jnp.concatenate([positions.reshape(3 * leaves, LEAF), charge], axis=0)
    up = [(i, i + 1) for i in range(devices - 1)]
    prev = lax.ppermute(stacked, AXES, up)
    after = lax.ppermute(stacked, AXES, [(j, i) for i, j in up])

    counts_row = counts.reshape(1, leaves)
    dense_max = leaves * LEAF + ROWS
    nodes_dev = leaves + leaves // 8
    basis, nodes, outgoing, sel = pl.pallas_call(
        up_kernel,
        out_shape=(
            jax.ShapeDtypeStruct((dense_max, MP), BF),
            jax.ShapeDtypeStruct((nodes_dev, MP), BF),
            jax.ShapeDtypeStruct((SHIFTS * CAP, MP), BF),
            jax.ShapeDtypeStruct((REACH * CAP, MP), BF),
        ),
        in_specs=[SM, SM, SM, VM, VM, VM, VM, VM, VM],
        out_specs=(VM, VM, VM, VM),
        scratch_shapes=[
            pltpu.VMEM((dense_max + LEAF, 32), F32),
            pltpu.VMEM((leaves, MP), F32),
            pltpu.VMEM((2, leaves, LEAF), F32),
        ],
        compiler_params=pltpu.CompilerParams(vmem_limit_bytes=40 * MIB),
        cost_estimate=pl.CostEstimate(flops=10**9, bytes_accessed=10**7, transcendentals=4 * 10**6),
        name="upward",
    )(
        counts, centres.reshape(3 * leaves), high, stacked, counts_row, freqs, phases.reshape(1, MP), m2m,
        send_nodes.reshape(SHIFTS * CAP, 1),
    )

    across = []
    for i in range(devices):
        x, y = i // n_gy, i % n_gy
        to = x + 1 if y >= n_gy // 2 else x - 1
        if 0 <= to < n_gx:
            across.append((i, to * n_gy + y))
    recv = lax.ppermute(sel, AXES, across)
    slots = pl.pallas_call(
        slots_kernel,
        out_shape=jax.ShapeDtypeStruct((2 * SHIFTS * CAP, MP), BF),
        in_specs=[SM, VM, VM],
        out_specs=VM,
        name="slots",
    )(gy, outgoing, recv)
    got = lax.all_to_all(slots.reshape(n_gy, 2 * CAP, MP), "gy", 0, 0).reshape(2 * SHIFTS * CAP, MP)

    near = pl.pallas_call(
        near_kernel,
        out_shape=jax.ShapeDtypeStruct((leaves, LEAF), F32),
        in_specs=[SM, SM, VM, VM, VM, VM],
        out_specs=VM,
        scratch_shapes=[
            pltpu.VMEM((3 * leaves * 16, LEAF), BF),
            pltpu.VMEM((3 * leaves * 8, LEAF), F32),
            pltpu.VMEM((leaves * LEAF, 48), BF),
            pltpu.VMEM((leaves * LEAF + NEAR_BIG, LEAF), F32),
            pltpu.SMEM((2 * leaves + 16,), jnp.int32),
            pltpu.SMEM((2 * leaves + 16,), jnp.int32),
        ],
        compiler_params=pltpu.CompilerParams(vmem_limit_bytes=40 * MIB),
        cost_estimate=pl.CostEstimate(flops=5 * 10**9, bytes_accessed=10**6, transcendentals=4 * 10**7),
        name="near",
    )(counts, u_source.reshape(leaves * ULIST), prev, stacked, after, u_source)

    table_rows = 3 * MP
    out = pl.pallas_call(
        down_kernel,
        out_shape=jax.ShapeDtypeStruct((leaves, LEAF), F32),
        in_specs=[SM, SM, VM, VM, VM, VM, VM, VM, VM, HBM, HBM],
        out_specs=VM,
        scratch_shapes=[
            pltpu.VMEM((OFFSETS * MP, MP), BF),
            pltpu.VMEM((dense_max, MP), BF),
            pltpu.VMEM((table_rows, MP), BF),
            pltpu.VMEM((leaves, MP), jnp.int32),
            pltpu.VMEM((leaves, MP), jnp.int32),
            pltpu.VMEM((GROUP * OFFSETS, table_rows), BF),
            pltpu.VMEM((2, leaves * OFFSETS, LEAF), F32),
            pltpu.VMEM((leaves, MP), F32),
            pltpu.VMEM((dense_max // LEAF + 2, LEAF), F32),
            pltpu.SemaphoreType.DMA((2,)),
        ],
        compiler_params=pltpu.CompilerParams(vmem_limit_bytes=56 * MIB),
        cost_estimate=pl.CostEstimate(flops=2 * 10**10, bytes_accessed=2 * 10**7, transcendentals=0),
        name="downward",
    )(
        counts, gy, counts_row, counts.reshape(leaves, 1), nodes, got, v_source, v_offset, near,
        m2l.reshape(OFFSETS * MP, MP), basis,
    )
    return out.reshape(leaves * LEAF)


def solution(mesh):
    both = P(AXES)
    cols = P(None, AXES)
    in_specs = (
        cols, both, both, cols, P(), P(), P(), P(), P(AXES, None, None), P(AXES, None), P(AXES, None), P(AXES, None),
    )
    return jax.shard_map(per_device, mesh=mesh, in_specs=in_specs, out_specs=both, check_vma=False)
```

```python
import functools
import math

import jax
import jax.numpy as jnp
import numpy as np
from jax import lax
from jax.experimental import pallas as pl
from jax.experimental.pallas import tpu as pltpu
from jax.sharding import PartitionSpec as P

F32 = jnp.float32
BF = jnp.bfloat16
MP = 256
LEAF = 128
OFFSETS = 64
VLIST = 189
VPAD = 192
ULIST = 27
CAP = 32
REACH = 8
SHIFTS = 16
AXES = ("gx", "gy")
ROWS = 256
STEP = 512
MIB = 2**20
SM = pl.BlockSpec(memory_space=pltpu.SMEM)
HBM = pl.BlockSpec(memory_space=pl.ANY)


def block(value):
    return pl.BlockSpec(value.shape, lambda i: (0,) * len(value.shape))


NT = (((1,), (1,)), ((), ()))


def sine_coefficients(terms=4):
    f = 0.5 * np.cos(np.pi * (np.arange(400) + 0.5) / 800)
    target = math.sqrt(2.0) * np.sin(np.pi * f)
    basis = np.stack([f ** (2 * k + 1) for k in range(terms)], axis=1)
    return [float(c) for c in np.linalg.lstsq(basis, target, rcond=None)[0]]


SINE = sine_coefficients()


def rounded(v):
    return v.astype(BF).astype(F32)


def split3(v):
    a = rounded(v)
    b = rounded(v - a)
    return a, b, v - a - b


def pick3(rows, x, y, z):
    m = rows % 3
    return jnp.where(m == 0, x, jnp.where(m == 1, y, z))


def dot(a, b):
    return jnp.dot(a, b, preferred_element_type=F32)


def dense_rows(count):
    return (count + 7) & -8


def column(row):
    leaves = row.shape[1]
    sub = lax.broadcasted_iota(jnp.int32, (leaves, leaves), 0)
    lane = lax.broadcasted_iota(jnp.int32, (leaves, leaves), 1)
    return jnp.sum(jnp.where(lane == sub, row.astype(F32), 0.0), axis=1, keepdims=True).astype(jnp.int32)


def row_ranges(counts_row):
    leaves = counts_row.shape[1]
    sub = lax.broadcasted_iota(jnp.int32, (leaves, leaves), 0)
    lane = lax.broadcasted_iota(jnp.int32, (leaves, leaves), 1)
    size = jnp.broadcast_to(dense_rows(counts_row), (leaves, leaves)).astype(F32)
    first = jnp.sum(jnp.where(lane < sub, size, 0.0), axis=1, keepdims=True)
    last = jnp.sum(jnp.where(lane <= sub, size, 0.0), axis=1, keepdims=True)
    return first.astype(jnp.int32), last.astype(jnp.int32)


def up_kernel(
    counts_ref, centres_ref, gy_ref, stacked_ref, counts_row_ref, freqs_ref, phases_ref, send_ref, m2m_hbm,
    basis_hbm, nodes_ref, slots_ref, sel_ref, dense, total, mult, basis, m2m, chosen_rows, sems,
):
    leaves = counts_row_ref.shape[1]
    m2m_copy = pltpu.make_async_copy(m2m_hbm, m2m, sems.at[2])
    m2m_copy.start()
    rows = lax.broadcasted_iota(jnp.int32, (32, LEAF), 0)

    def pack(l, off):
        part = [jnp.broadcast_to(stacked_ref[pl.ds(c * leaves + l, 1), :], (32, LEAF)) for c in range(4)]
        rel = pick3(rows, *[part[c] - centres_ref[c * leaves + l] for c in range(3)])
        a, b, c = split3(rel)
        full = jnp.where(
            rows < 9, a,
            jnp.where(rows < 15, b, jnp.where(rows < 18, c, jnp.where(rows < 21, 1.0, jnp.where(rows == 24, part[3], 0.0)))),
        )
        dense[pl.ds(pl.multiple_of(off, 8), LEAF), :] = full.T
        return off + dense_rows(counts_ref[l])

    def pack8(i, off):
        for k in range(8):
            off = pack(i * 8 + k, off)
        return off

    used = lax.fori_loop(0, leaves // 8, pack8, jnp.int32(0))
    dense[pl.ds(pl.multiple_of(used, 8), STEP), :] = jnp.zeros((STEP, 32), F32)

    wide_rows = lax.broadcasted_iota(jnp.int32, (32, MP), 0)
    turn = pick3(wide_rows, *[jnp.broadcast_to(freqs_ref[c:c + 1, :], (32, MP)) for c in range(3)])
    turn = jnp.where(wide_rows < 18, turn, jnp.broadcast_to(phases_ref[...], (32, MP))) * (0.5 / math.pi)
    a, b, c = split3(turn)
    g = wide_rows // 3
    weights = jnp.where(
        wide_rows < 18,
        jnp.where((g == 0) | (g == 3) | (g == 5), a, jnp.where((g == 1) | (g == 4), b, c)),
        jnp.where(wide_rows == 18, a, jnp.where(wide_rows == 19, b, jnp.where(wide_rows == 20, c, 0.0))),
    ).astype(BF)

    first, last = row_ranges(counts_row_ref[...])
    lane = lax.broadcasted_iota(jnp.int32, (leaves, ROWS), 1)
    total[...] = jnp.zeros_like(total)

    def written(i, slot):
        place = pl.ds(pl.multiple_of(i * STEP, STEP), STEP)
        return pltpu.make_async_copy(basis.at[slot], basis_hbm.at[place, :], sems.at[slot])

    def step(i, _):
        slot = lax.rem(i, 2)

        @pl.when(i >= 2)
        def _():
            written(i - 2, slot).wait()

        sums = []
        for part in range(STEP // ROWS):
            base = pl.multiple_of(i * STEP + part * ROWS, ROWS)
            rel = dense[pl.ds(base, ROWS), :]
            turns = dot(rel.astype(BF), weights)
            f = turns - jnp.round(turns)
            u = f * f
            s = SINE[3]
            for k in (2, 1, 0):
                s = s * u + SINE[k]
            s = s * f
            value = 1.0 - s * s
            basis[slot, part * ROWS:(part + 1) * ROWS, :] = value.astype(BF)
            w = value * rel[:, 24:25]
            hi = w.astype(BF)
            lo = (w - hi.astype(F32)).astype(BF)
            member = ((lane >= first - base) & (lane < last - base)).astype(F32).astype(BF)
            sums.append(dot(member, hi) + dot(member, lo))
        total[...] += sums[0] + sums[1]
        written(i, slot).start()
        return 0

    steps = (used + STEP - 1) // STEP
    lax.fori_loop(0, steps, step, 0)
    leaf_mult = (total[...] * LEAF ** (-0.5)).astype(BF)
    for h in range(2):
        mult[h, :, :] = leaf_mult[:, h * LEAF:(h + 1) * LEAF].astype(F32)
    parents = leaves // 8
    parent = jnp.zeros((parents, MP), F32)
    m2m_copy.wait()
    for c in range(8):
        child = jnp.concatenate([mult[h, pl.ds(c, parents, stride=8), :] for h in range(2)], axis=1)
        parent += dot(child.astype(BF), m2m[c])
    nodes_ref[0:leaves, :] = leaf_mult
    nodes_ref[leaves:leaves + parents, :] = parent.astype(BF)
    ids = lax.broadcasted_iota(jnp.int32, (CAP, leaves + parents), 1).astype(F32)
    wanted = send_ref[...].astype(F32).T
    chosen = jnp.concatenate([(wanted[:, s:s + 1] == ids).astype(F32) for s in range(SHIFTS)], axis=0).astype(BF)
    chosen_rows[...] = dot(chosen, nodes_ref[...]).astype(BF)

    gy = gy_ref[0]
    high = gy >= SHIFTS // 2

    def rows_of(b):
        return chosen_rows[pl.ds(pl.multiple_of(b * CAP, CAP), CAP), :]

    for t in range(SHIFTS):
        for sub in range(2):
            b = ((t - gy) if sub == 0 else (gy - t)) - 1
            valid = (b >= 0) & (b < REACH)
            value = rows_of(sub * REACH + jnp.clip(b, 0, REACH - 1))
            slots_ref[pl.ds((2 * t + sub) * CAP, CAP), :] = jnp.where(valid, value, jnp.zeros_like(value))
    for t in range(SHIFTS // 2):
        b = jnp.where(high, t - gy + SHIFTS - 1, gy - t + SHIFTS // 2 - 1)
        value = rows_of(jnp.where(high, 0, REACH) + jnp.clip(b, 0, REACH - 1))
        sel_ref[pl.ds(t * CAP, CAP), :] = jnp.where(b < REACH, value, jnp.zeros_like(value))
    if_two = steps >= 2

    @pl.when(if_two)
    def _():
        written(steps - 2, lax.rem(steps - 2, 2)).wait()

    written(steps - 1, lax.rem(steps - 1, 2)).wait()


NEAR_BIG, NEAR_SMALL = 64, 32


def near_kernel(
    begin, end, counts_ref, us_ref, prev_ref, own_ref, next_ref, usv_ref,
    near_ref, feat, charge, tgt, acc_ref, big, small,
):
    leaves = own_ref.shape[0] // 4
    rows = lax.broadcasted_iota(jnp.int32, (8, LEAF), 0)

    def coords(ref, l):
        return [jnp.broadcast_to(ref[pl.ds(c * leaves + l, 1), :] - 2.0, (8, LEAF)) for c in range(3)]

    for part, ref in enumerate((prev_ref, own_ref, next_ref)):

        def build(i, _, part=part, ref=ref):
            for k in range(8):
                l = i * 8 + k
                x, y, z = coords(ref, l)
                n1, n2, n3 = split3(x * x + y * y + z * z)
                s1, s2, s3 = split3(-2.0 * pick3(rows, x, y, z))
                a = jnp.where(rows < 3, s1, jnp.where(rows < 6, s2, jnp.where(rows == 6, n1, n2)))
                b = jnp.where(rows < 3, s3, jnp.where(rows == 3, n3, 1.0))
                s = part * leaves + l
                feat[pl.ds(pl.multiple_of(s * 16, 16), 16), :] = jnp.concatenate([a, b], axis=0).astype(BF)
                charge[pl.ds(pl.multiple_of(s * 8, 8), 8), :] = jnp.broadcast_to(
                    ref[pl.ds(3 * leaves + l, 1), :], (8, LEAF)
                )
            return 0

        lax.fori_loop(0, leaves // 8, build, 0)

    def targets(i, _):
        for k in range(8):
            l = i * 8 + k
            x, y, z = coords(own_ref, l)
            n1, n2, n3 = split3(x * x + y * y + z * z + 0.01)
            s1, s2, s3 = split3(pick3(rows, x, y, z))
            zero = jnp.zeros_like(x)
            a1 = jnp.where(rows < 6, s1, 1.0)
            tail = jnp.where(rows == 5, n1, jnp.where(rows == 6, n2, n3))
            b1 = jnp.where(rows < 3, s1, jnp.where(rows == 3, 1.0, jnp.where(rows == 4, 0.0, tail)))
            a2 = jnp.where(rows < 6, s2, 0.0)
            a3 = jnp.where(rows < 3, s3, 0.0)
            full = jnp.concatenate([a1, b1, a2, zero, a3, zero], axis=0)
            tgt[pl.ds(pl.multiple_of(l * LEAF, LEAF), LEAF), :] = full.T.astype(BF)
        return 0

    lax.fori_loop(begin // 8, end // 8, targets, 0)

    def listing(l, state):
        n, m = state
        count = counts_ref[l]
        for c in range(LEAF // NEAR_BIG):
            left = count - c * NEAR_BIG
            place = l * LEAF + c * NEAR_BIG
            big[n] = place
            n = n + (left > NEAR_SMALL).astype(jnp.int32)
            small[m] = place
            m = m + ((left > 0) & (left <= NEAR_SMALL)).astype(jnp.int32)
        return n, m

    n_big, n_small = lax.fori_loop(begin, end, listing, (jnp.int32(0), jnp.int32(0)))

    def run(items, n, size, unroll):
        for k in range(unroll):
            items[n + k] = leaves * LEAF

        def work(i, _):
            for k in range(unroll):
                place = items[i * unroll + k]
                safe = jnp.minimum(place, leaves * LEAF - NEAR_BIG)
                l = safe >> 7
                lhs = tgt[pl.ds(pl.multiple_of(safe, NEAR_SMALL), size), :]
                acc = None
                for u in range(0, ULIST, 2):
                    two = [us_ref[v * leaves + l] for v in range(u, min(u + 2, ULIST))]
                    f = [feat[pl.ds(pl.multiple_of(s * 16, 16), 16), :] for s in two]
                    f = jnp.concatenate(f, axis=1) if len(f) > 1 else f[0]
                    r = lax.rsqrt(dot(lhs, jnp.concatenate([f, f, f], axis=0)))
                    for j, s in enumerate(two):
                        q = charge[pl.ds(pl.multiple_of(s * 8, 8), 8), :]
                        term = r[:, j * LEAF:(j + 1) * LEAF].reshape(size // 8, 8, LEAF) * q[None]
                        acc = term if acc is None else acc + term
                acc_ref[pl.ds(pl.multiple_of(place, NEAR_SMALL), size), :] = acc.reshape(size, LEAF)
            return 0

        lax.fori_loop(0, (n + unroll - 1) // unroll, work, 0)

    run(big, n_big, NEAR_BIG, 8)
    run(small, n_small, NEAR_SMALL, 8)

    def reduce(i, _):
        parts = []
        for k in range(8):
            l = i * 8 + k
            t = acc_ref[pl.ds(pl.multiple_of(l * LEAF, LEAF), LEAF), :].T
            parts.append(jnp.sum(t, axis=0, keepdims=True))
        near_ref[pl.ds(pl.multiple_of(i * 8 - begin, 8), 8), :] = jnp.concatenate(parts, axis=0)
        return 0

    lax.fori_loop(begin // 8, end // 8, reduce, 0)
    own_id = lax.broadcasted_iota(jnp.int32, usv_ref.shape, 1) + leaves
    times = column(jnp.sum((usv_ref[...] == own_id).astype(F32), axis=0, keepdims=True)).astype(F32)
    itself = own_ref[3 * leaves + begin:3 * leaves + end, :] * lax.rsqrt(jnp.full((1, LEAF), 0.01, F32))
    near_ref[...] = (near_ref[...] - times[begin:end] * itself) * (ULIST * LEAF) ** (-0.5)


GROUP = 16
SPREAD = 4


def down_kernel(
    counts_ref, gy_ref, counts_row_ref, nodes_ref, got_ref, vs_ref, vo_ref, near_ref, m2l_hbm, basis_hbm,
    pot_ref, m2l, basis, table, source, offset, tally, summed, local, far, sems,
):
    leaves = counts_row_ref.shape[1]
    m2l_copy = pltpu.make_async_copy(m2l_hbm, m2l, sems.at[0])
    basis_copy = pltpu.make_async_copy(basis_hbm, basis, sems.at[1])
    m2l_copy.start()
    basis_copy.start()
    gy = gy_ref[0]
    own = nodes_ref.shape[0]
    table[0:own, :] = nodes_ref[...]
    for s in range(SHIFTS):
        by = s + 1 if s < REACH else REACH - 1 - s
        block = 2 * ((gy - by) & (SHIFTS - 1)) + (0 if by > 0 else 1)
        table[own + s * CAP:own + (s + 1) * CAP, :] = got_ref[pl.ds(pl.multiple_of(block * CAP, CAP), CAP), :]
    top = own + SHIFTS * CAP
    table[top:, :] = jnp.zeros((table.shape[0] - top, MP), BF)
    offset[...] = jnp.full_like(offset, -1)
    offset[:, 0:VLIST] = vo_ref[...].astype(F32).T
    tally[...] = jnp.zeros_like(tally)
    source[...] = jnp.full_like(source, -1)
    source[:, 0:VLIST] = vs_ref[...].astype(F32).T
    sub = lax.broadcasted_iota(jnp.int32, (MP, MP), 0).astype(F32).astype(BF)
    one, zero = jnp.ones((), BF), jnp.zeros((), BF)
    F8 = jnp.float8_e4m3fn

    def group(g, _):
        for k in range(GROUP):
            l = g * GROUP + k
            o_row = offset[pl.ds(l, 1), :].astype(BF)
            o_hot = jnp.where(sub[0:OFFSETS] == o_row, one, zero).astype(F8)
            s_row = source[pl.ds(l, 1), :]
            for t in range(3):
                size = MP if t < 2 else 160
                part = jnp.clip(s_row - t * MP, -1.0, MP + 0.0).astype(BF)
                s_hot = jnp.where(sub[0:size] == part, one, zero).astype(F8)
                tally[k * OFFSETS:(k + 1) * OFFSETS, t * MP:t * MP + size] = lax.dot_general(
                    o_hot, s_hot, NT, preferred_element_type=F32
                ).astype(BF)
        both = dot(tally[...], table[...]).reshape(GROUP, OFFSETS, MP)
        summed[:, pl.ds(pl.multiple_of(g * GROUP, GROUP), GROUP), :] = jnp.swapaxes(both, 0, 1).astype(BF)
        return 0

    lax.fori_loop(0, leaves // GROUP, group, 0)
    m2l_copy.wait()
    local[...] = jnp.zeros_like(local)

    def translate(i, _):
        parts = [summed[i * 8 + k] for k in range(8)]
        local[...] += dot(jnp.concatenate(parts, axis=1), m2l[pl.ds(pl.multiple_of(i * 8 * MP, 8 * MP), 8 * MP), :])
        return 0

    lax.fori_loop(0, OFFSETS // 8, translate, 0)
    hi = local[...].astype(BF)
    lo = (local[...] - hi.astype(F32)).astype(BF)
    both = jnp.concatenate([hi, lo], axis=0)
    first, last = row_ranges(counts_row_ref[...])
    used = lax.fori_loop(0, leaves, lambda l, off: off + dense_rows(counts_ref[l]), jnp.int32(0))
    lane = lax.broadcasted_iota(jnp.int32, (leaves, ROWS), 1)
    basis_copy.wait()

    def expand(i, _):
        for part in range(SPREAD):
            j = i * SPREAD + part
            base = pl.multiple_of(j * ROWS, ROWS)
            p = lax.dot_general(both, basis[pl.ds(base, ROWS), :], NT, preferred_element_type=F32)
            p = p[:leaves] + p[leaves:]
            member = (lane >= first - base) & (lane < last - base)
            value = jnp.sum(jnp.where(member, p, 0.0), axis=0, keepdims=True)
            far[pl.ds(2 * j, 1), :] = value[:, :LEAF]
            far[pl.ds(2 * j + 1, 1), :] = value[:, LEAF:]
        return 0

    lax.fori_loop(0, (used + SPREAD * ROWS - 1) // (SPREAD * ROWS), expand, 0)
    lane1 = lax.broadcasted_iota(jnp.int32, (1, LEAF), 1)

    def place(i, off):
        parts = []
        for k in range(8):
            l = i * 8 + k
            row, at = off >> 7, off & (LEAF - 1)
            shift = (LEAF - at) & (LEAF - 1)
            a = pltpu.roll(far[pl.ds(row, 1), :], shift, 1)
            b = pltpu.roll(far[pl.ds(row + 1, 1), :], shift, 1)
            parts.append(jnp.where(lane1 < LEAF - at, a, b))
            off = off + dense_rows(counts_ref[l])
        pot_ref[pl.ds(pl.multiple_of(i * 8, 8), 8), :] = jnp.concatenate(parts, axis=0)
        return off

    lax.fori_loop(0, leaves // 8, place, jnp.int32(0))
    lane = lax.broadcasted_iota(jnp.int32, (leaves, LEAF), 1)
    value = pot_ref[...] * MP ** (-0.5) + near_ref[...]
    pot_ref[...] = jnp.where(lane < column(counts_row_ref[...]), value, 0.0)


def per_device(
    positions, charges, counts, centres, freqs, phases, m2m, m2l, send_nodes, v_source, v_offset, u_source
):
    leaves = counts.shape[0]
    n_gx, n_gy = lax.axis_size("gx"), lax.axis_size("gy")
    devices = n_gx * n_gy
    gy = lax.axis_index("gy").astype(jnp.int32).reshape(1)
    live = jnp.arange(LEAF, dtype=jnp.int32)[None, :] < counts[:, None]
    charge = jnp.where(live, charges.reshape(leaves, LEAF), 0.0)
    stacked = jnp.concatenate([positions.reshape(3 * leaves, LEAF), charge], axis=0)
    up = [(i, i + 1) for i in range(devices - 1)]
    prev = lax.ppermute(stacked, AXES, up)
    after = lax.ppermute(stacked, AXES, [(j, i) for i, j in up])

    counts_row = counts.reshape(1, leaves)
    dense_max = leaves * LEAF
    nodes_dev = leaves + leaves // 8
    limit = pltpu.CompilerParams(vmem_limit_bytes=60 * MIB)
    shape = jax.ShapeDtypeStruct
    vectors = (stacked, counts_row, freqs, phases.reshape(1, MP), send_nodes.reshape(SHIFTS, CAP))
    made = (
        shape((dense_max, MP), BF),
        shape((nodes_dev, MP), BF),
        shape((2 * SHIFTS * CAP, MP), BF),
        shape((REACH * CAP, MP), BF),
    )
    basis, nodes, slots, sel = pl.pallas_call(
        up_kernel,
        grid=(1,),
        out_shape=made,
        in_specs=[SM, SM, SM] + [block(v) for v in vectors] + [HBM],
        out_specs=[HBM] + [block(v) for v in made[1:]],
        scratch_shapes=[
            pltpu.VMEM((dense_max + STEP + LEAF, 32), F32),
            pltpu.VMEM((leaves, MP), F32),
            pltpu.VMEM((2, leaves, LEAF), F32),
            pltpu.VMEM((2, STEP, MP), BF),
            pltpu.VMEM(m2m.shape, BF),
            pltpu.VMEM((SHIFTS * CAP, MP), BF),
            pltpu.SemaphoreType.DMA((3,)),
        ],
        compiler_params=limit,
        cost_estimate=pl.CostEstimate(flops=10**9, bytes_accessed=10**7, transcendentals=4 * 10**6),
        name="upward",
    )(counts, centres.reshape(3 * leaves), gy, *vectors, m2m)

    across = []
    for i in range(devices):
        x, y = i // n_gy, i % n_gy
        to = x + 1 if y >= n_gy // 2 else x - 1
        if 0 <= to < n_gx:
            across.append((i, to * n_gy + y))
    recv = lax.ppermute(sel, AXES, across)

    nearby = (prev, stacked, after, u_source.T)

    def near_part(begin, end, cost):
        return pl.pallas_call(
            functools.partial(near_kernel, begin, end),
            grid=(1,),
            out_shape=shape((end - begin, LEAF), F32),
            in_specs=[SM, SM] + [block(v) for v in nearby],
            out_specs=pl.BlockSpec((end - begin, LEAF), lambda i: (0, 0)),
            scratch_shapes=[
                pltpu.VMEM((3 * leaves * 16, LEAF), BF),
                pltpu.VMEM((3 * leaves * 8, LEAF), F32),
                pltpu.VMEM((leaves * LEAF, 48), BF),
                pltpu.VMEM((leaves * LEAF + NEAR_BIG, LEAF), F32),
                pltpu.SMEM((2 * leaves + 16,), jnp.int32),
                pltpu.SMEM((2 * leaves + 16,), jnp.int32),
            ],
            compiler_params=limit,
            cost_estimate=pl.CostEstimate(flops=cost * 10**9, bytes_accessed=10**6, transcendentals=cost * 10**7),
            name="near",
        )(counts, u_source.T.reshape(leaves * ULIST), *nearby)

    low = (gy[0] < n_gy // 2).astype(jnp.int32)
    slots = lax.dynamic_update_slice(
        slots.reshape(n_gy, 2, CAP, MP), recv.reshape(n_gy // 2, 1, CAP, MP), (low * (n_gy // 2), low, 0, 0)
    )
    got = lax.all_to_all(slots.reshape(n_gy, 2 * CAP, MP), "gy", 0, 0).reshape(2 * SHIFTS * CAP, MP)
    near_all = near_part(0, leaves, 8)

    table_rows = 3 * MP
    vectors = (counts_row, nodes, got, v_source.T, v_offset.T, near_all)
    out = pl.pallas_call(
        down_kernel,
        grid=(1,),
        out_shape=shape((leaves, LEAF), F32),
        in_specs=[SM, SM] + [block(v) for v in vectors] + [HBM, HBM],
        out_specs=block(charge),
        scratch_shapes=[
            pltpu.VMEM((OFFSETS * MP, MP), BF),
            pltpu.VMEM((dense_max, MP), BF),
            pltpu.VMEM((table_rows, MP), BF),
            pltpu.VMEM((leaves, MP), F32),
            pltpu.VMEM((leaves, MP), F32),
            pltpu.VMEM((GROUP * OFFSETS, table_rows), BF),
            pltpu.VMEM((OFFSETS, leaves, MP), BF),
            pltpu.VMEM((leaves, MP), F32),
            pltpu.VMEM((dense_max // LEAF + 8, LEAF), F32),
            pltpu.SemaphoreType.DMA((2,)),
        ],
        compiler_params=limit,
        cost_estimate=pl.CostEstimate(flops=2 * 10**10, bytes_accessed=2 * 10**7, transcendentals=0),
        name="downward",
    )(counts, gy, *vectors, m2l.reshape(OFFSETS * MP, MP), basis)
    return out.reshape(leaves * LEAF)


def solution(mesh):
    both = P(AXES)
    cols = P(None, AXES)
    in_specs = (
        cols, both, both, cols, P(), P(), P(), P(), P(AXES, None, None), P(AXES, None), P(AXES, None), P(AXES, None),
    )
    return jax.shard_map(per_device, mesh=mesh, in_specs=in_specs, out_specs=both, check_vma=False)
```

```python
import functools
import math

import jax
import jax.numpy as jnp
import numpy as np
from jax import lax
from jax.experimental import pallas as pl
from jax.experimental.pallas import tpu as pltpu
from jax.sharding import PartitionSpec as P

F32 = jnp.float32
BF = jnp.bfloat16
MP = 256
LEAF = 128
OFFSETS = 64
VLIST = 189
VPAD = 192
ULIST = 27
CAP = 32
REACH = 8
SHIFTS = 16
AXES = ("gx", "gy")
ROWS = 256
STEP = 512
MIB = 2**20
SM = pl.BlockSpec(memory_space=pltpu.SMEM)
HBM = pl.BlockSpec(memory_space=pl.ANY)


def block(value):
    return pl.BlockSpec(value.shape, lambda i: (0,) * len(value.shape))


NT = (((1,), (1,)), ((), ()))


def sine_coefficients(terms=4):
    f = 0.5 * np.cos(np.pi * (np.arange(400) + 0.5) / 800)
    target = math.sqrt(2.0) * np.sin(np.pi * f)
    basis = np.stack([f ** (2 * k + 1) for k in range(terms)], axis=1)
    return [float(c) for c in np.linalg.lstsq(basis, target, rcond=None)[0]]


SINE = sine_coefficients()


def rounded(v):
    return v.astype(BF).astype(F32)


def split3(v):
    a = rounded(v)
    b = rounded(v - a)
    return a, b, v - a - b


def pick3(rows, x, y, z):
    m = rows % 3
    return jnp.where(m == 0, x, jnp.where(m == 1, y, z))


def dot(a, b):
    return jnp.dot(a, b, preferred_element_type=F32)


def dense_rows(count):
    return (count + 7) & -8


def column(row):
    leaves = row.shape[1]
    sub = lax.broadcasted_iota(jnp.int32, (leaves, leaves), 0)
    lane = lax.broadcasted_iota(jnp.int32, (leaves, leaves), 1)
    return jnp.sum(jnp.where(lane == sub, row.astype(F32), 0.0), axis=1, keepdims=True).astype(jnp.int32)


def row_ranges(counts_row):
    leaves = counts_row.shape[1]
    sub = lax.broadcasted_iota(jnp.int32, (leaves, leaves), 0)
    lane = lax.broadcasted_iota(jnp.int32, (leaves, leaves), 1)
    size = jnp.broadcast_to(dense_rows(counts_row), (leaves, leaves)).astype(F32)
    first = jnp.sum(jnp.where(lane < sub, size, 0.0), axis=1, keepdims=True)
    last = jnp.sum(jnp.where(lane <= sub, size, 0.0), axis=1, keepdims=True)
    return first.astype(jnp.int32), last.astype(jnp.int32)


def up_kernel(
    counts_ref, centres_ref, gy_ref, stacked_ref, counts_row_ref, freqs_ref, phases_ref, send_ref, m2m_hbm,
    basis_hbm, nodes_ref, slots_ref, sel_ref, dense, total, mult, basis, m2m, chosen_rows, sems,
):
    leaves = counts_row_ref.shape[1]
    m2m_copy = pltpu.make_async_copy(m2m_hbm, m2m, sems.at[2])
    m2m_copy.start()
    rows = lax.broadcasted_iota(jnp.int32, (32, LEAF), 0)

    def pack(l, off):
        part = [jnp.broadcast_to(stacked_ref[pl.ds(c * leaves + l, 1), :], (32, LEAF)) for c in range(4)]
        rel = pick3(rows, *[part[c] - centres_ref[c * leaves + l] for c in range(3)])
        a, b, c = split3(rel)
        full = jnp.where(
            rows < 9, a,
            jnp.where(rows < 15, b, jnp.where(rows < 18, c, jnp.where(rows < 21, 1.0, jnp.where(rows == 24, part[3], 0.0)))),
        )
        dense[pl.ds(pl.multiple_of(off, 8), LEAF), :] = full.T
        return off + dense_rows(counts_ref[l])

    def pack8(i, off):
        for k in range(8):
            off = pack(i * 8 + k, off)
        return off

    used = lax.fori_loop(0, leaves // 8, pack8, jnp.int32(0))
    dense[pl.ds(pl.multiple_of(used, 8), STEP), :] = jnp.zeros((STEP, 32), F32)

    wide_rows = lax.broadcasted_iota(jnp.int32, (32, MP), 0)
    turn = pick3(wide_rows, *[jnp.broadcast_to(freqs_ref[c:c + 1, :], (32, MP)) for c in range(3)])
    turn = jnp.where(wide_rows < 18, turn, jnp.broadcast_to(phases_ref[...], (32, MP))) * (0.5 / math.pi)
    a, b, c = split3(turn)
    g = wide_rows // 3
    weights = jnp.where(
        wide_rows < 18,
        jnp.where((g == 0) | (g == 3) | (g == 5), a, jnp.where((g == 1) | (g == 4), b, c)),
        jnp.where(wide_rows == 18, a, jnp.where(wide_rows == 19, b, jnp.where(wide_rows == 20, c, 0.0))),
    ).astype(BF)

    first, last = row_ranges(counts_row_ref[...])
    lane = lax.broadcasted_iota(jnp.int32, (leaves, ROWS), 1)
    total[...] = jnp.zeros_like(total)

    def written(i, slot):
        place = pl.ds(pl.multiple_of(i * STEP, STEP), STEP)
        return pltpu.make_async_copy(basis.at[slot], basis_hbm.at[place, :], sems.at[slot])

    def step(i, _):
        slot = lax.rem(i, 2)

        @pl.when(i >= 2)
        def _():
            written(i - 2, slot).wait()

        sums = []
        for part in range(STEP // ROWS):
            base = pl.multiple_of(i * STEP + part * ROWS, ROWS)
            rel = dense[pl.ds(base, ROWS), :]
            turns = dot(rel.astype(BF), weights)
            f = turns - jnp.round(turns)
            u = f * f
            s = SINE[3]
            for k in (2, 1, 0):
                s = s * u + SINE[k]
            s = s * f
            value = 1.0 - s * s
            basis[slot, part * ROWS:(part + 1) * ROWS, :] = value.astype(BF)
            w = value * rel[:, 24:25]
            hi = w.astype(BF)
            lo = (w - hi.astype(F32)).astype(BF)
            member = ((lane >= first - base) & (lane < last - base)).astype(F32).astype(BF)
            sums.append(dot(member, hi) + dot(member, lo))
        total[...] += sums[0] + sums[1]
        written(i, slot).start()
        return 0

    steps = (used + STEP - 1) // STEP
    lax.fori_loop(0, steps, step, 0)
    leaf_mult = (total[...] * LEAF ** (-0.5)).astype(BF)
    for h in range(2):
        mult[h, :, :] = leaf_mult[:, h * LEAF:(h + 1) * LEAF].astype(F32)
    parents = leaves // 8
    parent = jnp.zeros((parents, MP), F32)
    m2m_copy.wait()
    for c in range(8):
        child = jnp.concatenate([mult[h, pl.ds(c, parents, stride=8), :] for h in range(2)], axis=1)
        parent += dot(child.astype(BF), m2m[c])
    nodes_ref[0:leaves, :] = leaf_mult
    nodes_ref[leaves:leaves + parents, :] = parent.astype(BF)
    ids = lax.broadcasted_iota(jnp.int32, (CAP, leaves + parents), 1).astype(F32)
    wanted = send_ref[...].astype(F32).T
    chosen = jnp.concatenate([(wanted[:, s:s + 1] == ids).astype(F32) for s in range(SHIFTS)], axis=0).astype(BF)
    chosen_rows[...] = dot(chosen, nodes_ref[...]).astype(BF)

    gy = gy_ref[0]
    high = gy >= SHIFTS // 2

    def rows_of(b):
        return chosen_rows[pl.ds(pl.multiple_of(b * CAP, CAP), CAP), :]

    for t in range(SHIFTS):
        for sub in range(2):
            b = ((t - gy) if sub == 0 else (gy - t)) - 1
            valid = (b >= 0) & (b < REACH)
            value = rows_of(sub * REACH + jnp.clip(b, 0, REACH - 1))
            slots_ref[pl.ds((2 * t + sub) * CAP, CAP), :] = jnp.where(valid, value, jnp.zeros_like(value))
    for t in range(SHIFTS // 2):
        b = jnp.where(high, t - gy + SHIFTS - 1, gy - t + SHIFTS // 2 - 1)
        value = rows_of(jnp.where(high, 0, REACH) + jnp.clip(b, 0, REACH - 1))
        sel_ref[pl.ds(t * CAP, CAP), :] = jnp.where(b < REACH, value, jnp.zeros_like(value))
    if_two = steps >= 2

    @pl.when(if_two)
    def _():
        written(steps - 2, lax.rem(steps - 2, 2)).wait()

    written(steps - 1, lax.rem(steps - 1, 2)).wait()


NEAR_BIG, NEAR_SMALL = 64, 32


def near_kernel(
    begin, end, counts_ref, odd_ref, us_ref, evens_ref, own_ref, odds_ref, usv_ref,
    near_ref, feat, charge, tgt, acc_ref, big, small,
):
    leaves = own_ref.shape[0] // 4
    rows = lax.broadcasted_iota(jnp.int32, (8, LEAF), 0)

    def coords(ref, l):
        return [jnp.broadcast_to(ref[pl.ds(c * leaves + l, 1), :] - 2.0, (8, LEAF)) for c in range(3)]

    odd = odd_ref[0]
    for part, ref in ((2 * (1 - odd), evens_ref), (1, own_ref), (2 * odd, odds_ref)):

        def build(i, _, part=part, ref=ref):
            for k in range(8):
                l = i * 8 + k
                x, y, z = coords(ref, l)
                n1, n2, n3 = split3(x * x + y * y + z * z)
                s1, s2, s3 = split3(-2.0 * pick3(rows, x, y, z))
                a = jnp.where(rows < 3, s1, jnp.where(rows < 6, s2, jnp.where(rows == 6, n1, n2)))
                b = jnp.where(rows < 3, s3, jnp.where(rows == 3, n3, 1.0))
                s = part * leaves + l
                feat[s] = jnp.concatenate([a, b], axis=0).astype(BF)
                charge[s] = jnp.broadcast_to(
                    ref[pl.ds(3 * leaves + l, 1), :], (8, LEAF)
                )
            return 0

        lax.fori_loop(0, leaves // 8, build, 0)

    def targets(i, _):
        for k in range(8):
            l = i * 8 + k
            x, y, z = coords(own_ref, l)
            n1, n2, n3 = split3(x * x + y * y + z * z + 0.01)
            s1, s2, s3 = split3(pick3(rows, x, y, z))
            zero = jnp.zeros_like(x)
            a1 = jnp.where(rows < 6, s1, 1.0)
            tail = jnp.where(rows == 5, n1, jnp.where(rows == 6, n2, n3))
            b1 = jnp.where(rows < 3, s1, jnp.where(rows == 3, 1.0, jnp.where(rows == 4, 0.0, tail)))
            a2 = jnp.where(rows < 6, s2, 0.0)
            a3 = jnp.where(rows < 3, s3, 0.0)
            full = jnp.concatenate([a1, b1, a2, zero, a3, zero], axis=0)
            tgt[pl.ds(pl.multiple_of(l * LEAF, LEAF), LEAF), :] = full.T.astype(BF)
        return 0

    lax.fori_loop(begin // 8, end // 8, targets, 0)

    def listing(l, state):
        n, m = state
        count = counts_ref[l]
        for c in range(LEAF // NEAR_BIG):
            left = count - c * NEAR_BIG
            place = l * LEAF + c * NEAR_BIG
            big[n] = place
            n = n + (left > NEAR_SMALL).astype(jnp.int32)
            small[m] = place
            m = m + ((left > 0) & (left <= NEAR_SMALL)).astype(jnp.int32)
        return n, m

    n_big, n_small = lax.fori_loop(begin, end, listing, (jnp.int32(0), jnp.int32(0)), unroll=4)

    def run(items, n, size, unroll):
        for k in range(unroll):
            items[n + k] = leaves * LEAF

        def work(i, _):
            for k in range(unroll):
                place = items[i * unroll + k]
                safe = jnp.minimum(place, leaves * LEAF - NEAR_BIG)
                l = safe >> 7
                lhs = tgt[pl.ds(pl.multiple_of(safe, NEAR_SMALL), size), :]
                acc = None
                for u in range(0, ULIST, 2):
                    two = [us_ref[v * leaves + l] for v in range(u, min(u + 2, ULIST))]
                    f = [feat[s] for s in two]
                    f = jnp.concatenate(f, axis=1) if len(f) > 1 else f[0]
                    r = lax.rsqrt(dot(lhs, jnp.concatenate([f, f, f], axis=0)))
                    for j, s in enumerate(two):
                        q = charge[s]
                        term = r[:, j * LEAF:(j + 1) * LEAF].reshape(size // 8, 8, LEAF) * q[None]
                        acc = term if acc is None else acc + term
                acc_ref[pl.ds(pl.multiple_of(place, NEAR_SMALL), size), :] = acc.reshape(size, LEAF)
            return 0

        lax.fori_loop(0, (n + unroll - 1) // unroll, work, 0)

    run(big, n_big, NEAR_BIG, 8)
    run(small, n_small, NEAR_SMALL, 8)

    def reduce(i, _):
        parts = []
        for k in range(8):
            l = i * 8 + k
            t = acc_ref[pl.ds(pl.multiple_of(l * LEAF, LEAF), LEAF), :].T
            parts.append(jnp.sum(t, axis=0, keepdims=True))
        near_ref[pl.ds(pl.multiple_of(i * 8 - begin, 8), 8), :] = jnp.concatenate(parts, axis=0)
        return 0

    lax.fori_loop(begin // 8, end // 8, reduce, 0)
    own_id = lax.broadcasted_iota(jnp.int32, usv_ref.shape, 1) + leaves
    times = column(jnp.sum((usv_ref[...] == own_id).astype(F32), axis=0, keepdims=True)).astype(F32)
    itself = own_ref[3 * leaves + begin:3 * leaves + end, :] * lax.rsqrt(jnp.full((1, LEAF), 0.01, F32))
    near_ref[...] = (near_ref[...] - times[begin:end] * itself) * (ULIST * LEAF) ** (-0.5)


GROUP = 16
SPREAD = 4


def down_kernel(
    counts_ref, gy_ref, counts_row_ref, nodes_ref, got_ref, vs_ref, vo_ref, near_ref, m2l_hbm, basis_hbm,
    pot_ref, m2l, basis, table, source, offset, tally, summed, local, far, sems,
):
    leaves = counts_row_ref.shape[1]
    m2l_copy = pltpu.make_async_copy(m2l_hbm, m2l, sems.at[0])
    basis_copy = pltpu.make_async_copy(basis_hbm, basis, sems.at[1])
    m2l_copy.start()
    basis_copy.start()
    gy = gy_ref[0]
    own = nodes_ref.shape[0]
    table[0:own, :] = nodes_ref[...]
    for s in range(SHIFTS):
        by = s + 1 if s < REACH else REACH - 1 - s
        block = 2 * ((gy - by) & (SHIFTS - 1)) + (0 if by > 0 else 1)
        table[own + s * CAP:own + (s + 1) * CAP, :] = got_ref[pl.ds(pl.multiple_of(block * CAP, CAP), CAP), :]
    top = own + SHIFTS * CAP
    table[top:, :] = jnp.zeros((table.shape[0] - top, MP), BF)
    offset[...] = jnp.full_like(offset, -1)
    offset[:, 0:VLIST] = vo_ref[...].astype(F32).T
    tally[...] = jnp.zeros_like(tally)
    source[...] = jnp.full_like(source, -1)
    source[:, 0:VLIST] = vs_ref[...].astype(F32).T
    sub = lax.broadcasted_iota(jnp.int32, (MP, MP), 0).astype(F32).astype(BF)
    one, zero = jnp.ones((), BF), jnp.zeros((), BF)
    F8 = jnp.float8_e4m3fn

    def group(g, _):
        for k in range(GROUP):
            l = g * GROUP + k
            o_row = offset[pl.ds(l, 1), :].astype(BF)
            o_hot = jnp.where(sub[0:OFFSETS] == o_row, one, zero).astype(F8)
            s_row = source[pl.ds(l, 1), :]
            for t in range(3):
                size = MP if t < 2 else 160
                part = jnp.clip(s_row - t * MP, -1.0, MP + 0.0).astype(BF)
                s_hot = jnp.where(sub[0:size] == part, one, zero).astype(F8)
                tally[k * OFFSETS:(k + 1) * OFFSETS, t * MP:t * MP + size] = lax.dot_general(
                    o_hot, s_hot, NT, preferred_element_type=F32
                ).astype(BF)
        both = dot(tally[...], table[...]).reshape(GROUP, OFFSETS, MP)
        summed[:, pl.ds(pl.multiple_of(g * GROUP, GROUP), GROUP), :] = jnp.swapaxes(both, 0, 1).astype(BF)
        return 0

    lax.fori_loop(0, leaves // GROUP, group, 0)
    m2l_copy.wait()
    local[...] = jnp.zeros_like(local)

    def translate(i, _):
        parts = [summed[i * 8 + k] for k in range(8)]
        local[...] += dot(jnp.concatenate(parts, axis=1), m2l[pl.ds(pl.multiple_of(i * 8 * MP, 8 * MP), 8 * MP), :])
        return 0

    lax.fori_loop(0, OFFSETS // 8, translate, 0)
    hi = local[...].astype(BF)
    lo = (local[...] - hi.astype(F32)).astype(BF)
    both = jnp.concatenate([hi, lo], axis=0)
    first, last = row_ranges(counts_row_ref[...])
    used = lax.fori_loop(0, leaves, lambda l, off: off + dense_rows(counts_ref[l]), jnp.int32(0))
    lane = lax.broadcasted_iota(jnp.int32, (leaves, ROWS), 1)
    basis_copy.wait()

    def expand(i, _):
        for part in range(SPREAD):
            j = i * SPREAD + part
            base = pl.multiple_of(j * ROWS, ROWS)
            p = lax.dot_general(both, basis[pl.ds(base, ROWS), :], NT, preferred_element_type=F32)
            p = p[:leaves] + p[leaves:]
            member = (lane >= first - base) & (lane < last - base)
            value = jnp.sum(jnp.where(member, p, 0.0), axis=0, keepdims=True)
            far[pl.ds(2 * j, 1), :] = value[:, :LEAF]
            far[pl.ds(2 * j + 1, 1), :] = value[:, LEAF:]
        return 0

    lax.fori_loop(0, (used + SPREAD * ROWS - 1) // (SPREAD * ROWS), expand, 0)
    lane1 = lax.broadcasted_iota(jnp.int32, (1, LEAF), 1)

    def place(i, off):
        parts = []
        for k in range(8):
            l = i * 8 + k
            row, at = off >> 7, off & (LEAF - 1)
            shift = (LEAF - at) & (LEAF - 1)
            a = pltpu.roll(far[pl.ds(row, 1), :], shift, 1)
            b = pltpu.roll(far[pl.ds(row + 1, 1), :], shift, 1)
            parts.append(jnp.where(lane1 < LEAF - at, a, b))
            off = off + dense_rows(counts_ref[l])
        pot_ref[pl.ds(pl.multiple_of(i * 8, 8), 8), :] = jnp.concatenate(parts, axis=0)
        return off

    lax.fori_loop(0, leaves // 8, place, jnp.int32(0))
    lane = lax.broadcasted_iota(jnp.int32, (leaves, LEAF), 1)
    value = pot_ref[...] * MP ** (-0.5) + near_ref[...]
    pot_ref[...] = jnp.where(lane < column(counts_row_ref[...]), value, 0.0)


def per_device(
    positions, charges, counts, centres, freqs, phases, m2m, m2l, send_nodes, v_source, v_offset, u_source
):
    leaves = counts.shape[0]
    n_gx, n_gy = lax.axis_size("gx"), lax.axis_size("gy")
    devices = n_gx * n_gy
    gy = lax.axis_index("gy").astype(jnp.int32).reshape(1)
    live = jnp.arange(LEAF, dtype=jnp.int32)[None, :] < counts[:, None]
    charge = jnp.where(live, charges.reshape(leaves, LEAF), 0.0)
    stacked = jnp.concatenate([positions.reshape(3 * leaves, LEAF), charge], axis=0)
    def swapped(first):
        lower = range(first, devices - 1, 2)
        return lax.ppermute(stacked, AXES, [(i, i + 1) for i in lower] + [(i + 1, i) for i in lower])

    evens, odds = swapped(0), swapped(1)
    odd = gy & 1

    counts_row = counts.reshape(1, leaves)
    dense_max = leaves * LEAF
    nodes_dev = leaves + leaves // 8
    limit = pltpu.CompilerParams(vmem_limit_bytes=60 * MIB)
    shape = jax.ShapeDtypeStruct
    vectors = (stacked, counts_row, freqs, phases.reshape(1, MP), send_nodes.reshape(SHIFTS, CAP))
    made = (
        shape((dense_max, MP), BF),
        shape((nodes_dev, MP), BF),
        shape((2 * SHIFTS * CAP, MP), BF),
        shape((REACH * CAP, MP), BF),
    )
    basis, nodes, slots, sel = pl.pallas_call(
        up_kernel,
        grid=(1,),
        out_shape=made,
        in_specs=[SM, SM, SM] + [block(v) for v in vectors] + [HBM],
        out_specs=[HBM] + [block(v) for v in made[1:]],
        scratch_shapes=[
            pltpu.VMEM((dense_max + STEP + LEAF, 32), F32),
            pltpu.VMEM((leaves, MP), F32),
            pltpu.VMEM((2, leaves, LEAF), F32),
            pltpu.VMEM((2, STEP, MP), BF),
            pltpu.VMEM(m2m.shape, BF),
            pltpu.VMEM((SHIFTS * CAP, MP), BF),
            pltpu.SemaphoreType.DMA((3,)),
        ],
        compiler_params=limit,
        cost_estimate=pl.CostEstimate(flops=10**9, bytes_accessed=10**7, transcendentals=4 * 10**6),
        name="upward",
    )(counts, centres.reshape(3 * leaves), gy, *vectors, m2m)

    across = []
    for i in range(devices):
        x, y = i // n_gy, i % n_gy
        to = x + 1 if y >= n_gy // 2 else x - 1
        if 0 <= to < n_gx:
            across.append((i, to * n_gy + y))
    recv = lax.ppermute(sel, AXES, across)

    nearby = (evens, stacked, odds, u_source.T)

    def near_part(begin, end, cost):
        return pl.pallas_call(
            functools.partial(near_kernel, begin, end),
            grid=(1,),
            out_shape=shape((end - begin, LEAF), F32),
            in_specs=[SM, SM, SM] + [block(v) for v in nearby],
            out_specs=pl.BlockSpec((end - begin, LEAF), lambda i: (0, 0)),
            scratch_shapes=[
                pltpu.VMEM((3 * leaves, 16, LEAF), BF),
                pltpu.VMEM((3 * leaves, 8, LEAF), F32),
                pltpu.VMEM((leaves * LEAF, 48), BF),
                pltpu.VMEM((leaves * LEAF + NEAR_BIG, LEAF), F32),
                pltpu.SMEM((2 * leaves + 16,), jnp.int32),
                pltpu.SMEM((2 * leaves + 16,), jnp.int32),
            ],
            compiler_params=limit,
            cost_estimate=pl.CostEstimate(flops=cost * 10**9, bytes_accessed=10**6, transcendentals=cost * 10**7),
            name="near",
        )(counts, odd, u_source.T.reshape(leaves * ULIST), *nearby)

    low = (gy[0] < n_gy // 2).astype(jnp.int32)
    slots = lax.dynamic_update_slice(
        slots.reshape(n_gy, 2, CAP, MP), recv.reshape(n_gy // 2, 1, CAP, MP), (low * (n_gy // 2), low, 0, 0)
    )
    got = lax.all_to_all(slots.reshape(n_gy, 2 * CAP, MP), "gy", 0, 0).reshape(2 * SHIFTS * CAP, MP)
    near_all = near_part(0, leaves, 8)

    table_rows = 3 * MP
    vectors = (counts_row, nodes, got, v_source.T, v_offset.T, near_all)
    out = pl.pallas_call(
        down_kernel,
        grid=(1,),
        out_shape=shape((leaves, LEAF), F32),
        in_specs=[SM, SM] + [block(v) for v in vectors] + [HBM, HBM],
        out_specs=block(charge),
        scratch_shapes=[
            pltpu.VMEM((OFFSETS * MP, MP), BF),
            pltpu.VMEM((dense_max, MP), BF),
            pltpu.VMEM((table_rows, MP), BF),
            pltpu.VMEM((leaves, MP), F32),
            pltpu.VMEM((leaves, MP), F32),
            pltpu.VMEM((GROUP * OFFSETS, table_rows), BF),
            pltpu.VMEM((OFFSETS, leaves, MP), BF),
            pltpu.VMEM((leaves, MP), F32),
            pltpu.VMEM((dense_max // LEAF + 8, LEAF), F32),
            pltpu.SemaphoreType.DMA((2,)),
        ],
        compiler_params=limit,
        cost_estimate=pl.CostEstimate(flops=2 * 10**10, bytes_accessed=2 * 10**7, transcendentals=0),
        name="downward",
    )(counts, gy, *vectors, m2l.reshape(OFFSETS * MP, MP), basis)
    return out.reshape(leaves * LEAF)


def solution(mesh):
    both = P(AXES)
    cols = P(None, AXES)
    in_specs = (
        cols, both, both, cols, P(), P(), P(), P(), P(AXES, None, None), P(AXES, None), P(AXES, None), P(AXES, None),
    )
    return jax.shard_map(per_device, mesh=mesh, in_specs=in_specs, out_specs=both, check_vma=False)
```

```python
import functools
import math

import jax
import jax.numpy as jnp
import numpy as np
from jax import lax
from jax.experimental import pallas as pl
from jax.experimental.pallas import tpu as pltpu
from jax.sharding import PartitionSpec as P

F32 = jnp.float32
BF = jnp.bfloat16
MP = 256
LEAF = 128
OFFSETS = 64
VLIST = 189
VPAD = 192
ULIST = 27
CAP = 32
REACH = 8
SHIFTS = 16
AXES = ("gx", "gy")
ROWS = 256
STEP = 1024
MIB = 2**20
SM = pl.BlockSpec(memory_space=pltpu.SMEM)
HBM = pl.BlockSpec(memory_space=pl.ANY)


def block(value):
    return pl.BlockSpec(value.shape, lambda i: (0,) * len(value.shape))


NT = (((1,), (1,)), ((), ()))


def sine_coefficients(terms=4):
    f = 0.5 * np.cos(np.pi * (np.arange(400) + 0.5) / 800)
    target = math.sqrt(2.0) * np.sin(np.pi * f)
    basis = np.stack([f ** (2 * k + 1) for k in range(terms)], axis=1)
    return [float(c) for c in np.linalg.lstsq(basis, target, rcond=None)[0]]


SINE = sine_coefficients()


def rounded(v):
    return v.astype(BF).astype(F32)


def split3(v):
    a = rounded(v)
    b = rounded(v - a)
    return a, b, v - a - b


def pick3(rows, x, y, z):
    m = rows % 3
    return jnp.where(m == 0, x, jnp.where(m == 1, y, z))


def dot(a, b):
    return jnp.dot(a, b, preferred_element_type=F32)


def dense_rows(count):
    return (count + 7) & -8


def column(row):
    leaves = row.shape[1]
    sub = lax.broadcasted_iota(jnp.int32, (leaves, leaves), 0)
    lane = lax.broadcasted_iota(jnp.int32, (leaves, leaves), 1)
    return jnp.sum(jnp.where(lane == sub, row.astype(F32), 0.0), axis=1, keepdims=True).astype(jnp.int32)


def row_ranges(counts_row):
    leaves = counts_row.shape[1]
    sub = lax.broadcasted_iota(jnp.int32, (leaves, leaves), 0)
    lane = lax.broadcasted_iota(jnp.int32, (leaves, leaves), 1)
    size = jnp.broadcast_to(dense_rows(counts_row), (leaves, leaves)).astype(F32)
    first = jnp.sum(jnp.where(lane < sub, size, 0.0), axis=1, keepdims=True)
    last = jnp.sum(jnp.where(lane <= sub, size, 0.0), axis=1, keepdims=True)
    return first.astype(jnp.int32), last.astype(jnp.int32)


def up_kernel(
    counts_ref, centres_ref, gy_ref, stacked_ref, counts_row_ref, freqs_ref, phases_ref, send_ref, m2m_hbm,
    basis_hbm, nodes_ref, slots_ref, sel_ref, dense, total, mult, basis, m2m, chosen_rows, sems,
):
    leaves = counts_row_ref.shape[1]
    m2m_copy = pltpu.make_async_copy(m2m_hbm, m2m, sems.at[2])
    m2m_copy.start()
    rows = lax.broadcasted_iota(jnp.int32, (32, LEAF), 0)

    def pack(l, off):
        part = [jnp.broadcast_to(stacked_ref[pl.ds(c * leaves + l, 1), :], (32, LEAF)) for c in range(4)]
        rel = pick3(rows, *[part[c] - centres_ref[c * leaves + l] for c in range(3)])
        a, b, c = split3(rel)
        full = jnp.where(
            rows < 9, a,
            jnp.where(rows < 15, b, jnp.where(rows < 18, c, jnp.where(rows < 21, 1.0, jnp.where(rows == 24, part[3], 0.0)))),
        )
        dense[pl.ds(pl.multiple_of(off, 8), LEAF), :] = full.T
        return off + dense_rows(counts_ref[l])

    def pack8(i, off):
        for k in range(8):
            off = pack(i * 8 + k, off)
        return off

    used = lax.fori_loop(0, leaves // 8, pack8, jnp.int32(0))
    dense[pl.ds(pl.multiple_of(used, 8), STEP), :] = jnp.zeros((STEP, 32), F32)

    wide_rows = lax.broadcasted_iota(jnp.int32, (32, MP), 0)
    turn = pick3(wide_rows, *[jnp.broadcast_to(freqs_ref[c:c + 1, :], (32, MP)) for c in range(3)])
    turn = jnp.where(wide_rows < 18, turn, jnp.broadcast_to(phases_ref[...], (32, MP))) * (0.5 / math.pi)
    a, b, c = split3(turn)
    g = wide_rows // 3
    weights = jnp.where(
        wide_rows < 18,
        jnp.where((g == 0) | (g == 3) | (g == 5), a, jnp.where((g == 1) | (g == 4), b, c)),
        jnp.where(wide_rows == 18, a, jnp.where(wide_rows == 19, b, jnp.where(wide_rows == 20, c, 0.0))),
    ).astype(BF)

    first, last = row_ranges(counts_row_ref[...])
    lane = lax.broadcasted_iota(jnp.int32, (leaves, ROWS), 1)
    total[...] = jnp.zeros_like(total)

    def written(i, slot):
        place = pl.ds(pl.multiple_of(i * STEP, STEP), STEP)
        return pltpu.make_async_copy(basis.at[slot], basis_hbm.at[place, :], sems.at[slot])

    def step(i, _):
        slot = lax.rem(i, 2)

        @pl.when(i >= 2)
        def _():
            written(i - 2, slot).wait()

        sums = []
        for part in range(STEP // ROWS):
            base = pl.multiple_of(i * STEP + part * ROWS, ROWS)
            rel = dense[pl.ds(base, ROWS), :]
            turns = dot(rel.astype(BF), weights)
            f = turns - jnp.round(turns)
            u = f * f
            s = SINE[3]
            for k in (2, 1, 0):
                s = s * u + SINE[k]
            s = s * f
            value = 1.0 - s * s
            basis[slot, part * ROWS:(part + 1) * ROWS, :] = value.astype(BF)
            w = value * rel[:, 24:25]
            hi = w.astype(BF)
            lo = (w - hi.astype(F32)).astype(BF)
            member = ((lane >= first - base) & (lane < last - base)).astype(F32).astype(BF)
            sums.append(dot(member, hi) + dot(member, lo))
        total[...] += sum(sums)
        written(i, slot).start()
        return 0

    steps = (used + STEP - 1) // STEP
    lax.fori_loop(0, steps, step, 0)
    leaf_mult = (total[...] * LEAF ** (-0.5)).astype(BF)
    for h in range(2):
        mult[h, :, :] = leaf_mult[:, h * LEAF:(h + 1) * LEAF].astype(F32)
    parents = leaves // 8
    parent = jnp.zeros((parents, MP), F32)
    m2m_copy.wait()
    for c in range(8):
        child = jnp.concatenate([mult[h, pl.ds(c, parents, stride=8), :] for h in range(2)], axis=1)
        parent += dot(child.astype(BF), m2m[c])
    nodes_ref[0:leaves, :] = leaf_mult
    nodes_ref[leaves:leaves + parents, :] = parent.astype(BF)
    ids = lax.broadcasted_iota(jnp.int32, (CAP, leaves + parents), 1).astype(F32)
    wanted = send_ref[...].astype(F32).T
    chosen = jnp.concatenate([(wanted[:, s:s + 1] == ids).astype(F32) for s in range(SHIFTS)], axis=0).astype(BF)
    chosen_rows[...] = dot(chosen, nodes_ref[...]).astype(BF)

    gy = gy_ref[0]
    high = gy >= SHIFTS // 2

    def rows_of(b):
        return chosen_rows[pl.ds(pl.multiple_of(b * CAP, CAP), CAP), :]

    for t in range(SHIFTS):
        for sub in range(2):
            b = ((t - gy) if sub == 0 else (gy - t)) - 1
            valid = (b >= 0) & (b < REACH)
            value = rows_of(sub * REACH + jnp.clip(b, 0, REACH - 1))
            slots_ref[pl.ds((2 * t + sub) * CAP, CAP), :] = jnp.where(valid, value, jnp.zeros_like(value))
    for t in range(SHIFTS // 2):
        b = jnp.where(high, t - gy + SHIFTS - 1, gy - t + SHIFTS // 2 - 1)
        value = rows_of(jnp.where(high, 0, REACH) + jnp.clip(b, 0, REACH - 1))
        sel_ref[pl.ds(t * CAP, CAP), :] = jnp.where(b < REACH, value, jnp.zeros_like(value))
    if_two = steps >= 2

    @pl.when(if_two)
    def _():
        written(steps - 2, lax.rem(steps - 2, 2)).wait()

    written(steps - 1, lax.rem(steps - 1, 2)).wait()


NEAR_BIG, NEAR_SMALL = 64, 32


def near_kernel(
    begin, end, counts_ref, odd_ref, us_ref, evens_ref, own_ref, odds_ref, usv_ref,
    near_ref, feat, charge, tgt, acc_ref, big, small,
):
    leaves = own_ref.shape[0] // 4
    rows = lax.broadcasted_iota(jnp.int32, (8, LEAF), 0)

    def coords(ref, l):
        return [jnp.broadcast_to(ref[pl.ds(c * leaves + l, 1), :] - 2.0, (8, LEAF)) for c in range(3)]

    odd = odd_ref[0]
    for part, ref in ((2 * (1 - odd), evens_ref), (1, own_ref), (2 * odd, odds_ref)):

        def build(i, _, part=part, ref=ref):
            for k in range(8):
                l = i * 8 + k
                x, y, z = coords(ref, l)
                n1, n2, n3 = split3(x * x + y * y + z * z)
                s1, s2, s3 = split3(-2.0 * pick3(rows, x, y, z))
                a = jnp.where(rows < 3, s1, jnp.where(rows < 6, s2, jnp.where(rows == 6, n1, n2)))
                b = jnp.where(rows < 3, s3, jnp.where(rows == 3, n3, 1.0))
                s = part * leaves + l
                feat[s] = jnp.concatenate([a, b], axis=0).astype(BF)
                charge[s] = jnp.broadcast_to(
                    ref[pl.ds(3 * leaves + l, 1), :], (8, LEAF)
                )
            return 0

        lax.fori_loop(0, leaves // 8, build, 0)

    def targets(i, _):
        for k in range(8):
            l = i * 8 + k
            x, y, z = coords(own_ref, l)
            n1, n2, n3 = split3(x * x + y * y + z * z + 0.01)
            s1, s2, s3 = split3(pick3(rows, x, y, z))
            zero = jnp.zeros_like(x)
            a1 = jnp.where(rows < 6, s1, 1.0)
            tail = jnp.where(rows == 5, n1, jnp.where(rows == 6, n2, n3))
            b1 = jnp.where(rows < 3, s1, jnp.where(rows == 3, 1.0, jnp.where(rows == 4, 0.0, tail)))
            a2 = jnp.where(rows < 6, s2, 0.0)
            a3 = jnp.where(rows < 3, s3, 0.0)
            full = jnp.concatenate([a1, b1, a2, zero, a3, zero], axis=0)
            tgt[pl.ds(pl.multiple_of(l * LEAF, LEAF), LEAF), :] = full.T.astype(BF)
        return 0

    lax.fori_loop(begin // 8, end // 8, targets, 0)

    def listing(l, state):
        n, m = state
        count = counts_ref[l]
        for c in range(LEAF // NEAR_BIG):
            left = count - c * NEAR_BIG
            place = l * LEAF + c * NEAR_BIG
            big[n] = place
            n = n + (left > NEAR_SMALL).astype(jnp.int32)
            small[m] = place
            m = m + ((left > 0) & (left <= NEAR_SMALL)).astype(jnp.int32)
        return n, m

    n_big, n_small = lax.fori_loop(begin, end, listing, (jnp.int32(0), jnp.int32(0)), unroll=4)

    def run(items, n, size, unroll):
        for k in range(unroll):
            items[n + k] = leaves * LEAF

        def work(i, _):
            for k in range(unroll):
                place = items[i * unroll + k]
                safe = jnp.minimum(place, leaves * LEAF - NEAR_BIG)
                l = safe >> 7
                lhs = tgt[pl.ds(pl.multiple_of(safe, NEAR_SMALL), size), :]
                acc = None
                for u in range(0, ULIST, 2):
                    two = [us_ref[v * leaves + l] for v in range(u, min(u + 2, ULIST))]
                    f = [feat[s] for s in two]
                    f = jnp.concatenate(f, axis=1) if len(f) > 1 else f[0]
                    r = lax.rsqrt(dot(lhs, jnp.concatenate([f, f, f], axis=0)))
                    for j, s in enumerate(two):
                        q = charge[s]
                        term = r[:, j * LEAF:(j + 1) * LEAF].reshape(size // 8, 8, LEAF) * q[None]
                        acc = term if acc is None else acc + term
                acc_ref[pl.ds(pl.multiple_of(place, NEAR_SMALL), size), :] = acc.reshape(size, LEAF)
            return 0

        lax.fori_loop(0, (n + unroll - 1) // unroll, work, 0)

    run(big, n_big, NEAR_BIG, 8)
    run(small, n_small, NEAR_SMALL, 8)

    def reduce(i, _):
        parts = []
        for k in range(16):
            l = i * 16 + k
            t = acc_ref[pl.ds(pl.multiple_of(l * LEAF, LEAF), LEAF), :].T
            parts.append(jnp.sum(t, axis=0, keepdims=True))
        near_ref[pl.ds(pl.multiple_of(i * 16 - begin, 16), 16), :] = jnp.concatenate(parts, axis=0)
        return 0

    lax.fori_loop(begin // 16, end // 16, reduce, 0)
    own_id = lax.broadcasted_iota(jnp.int32, usv_ref.shape, 1) + leaves
    times = column(jnp.sum((usv_ref[...] == own_id).astype(F32), axis=0, keepdims=True)).astype(F32)
    itself = own_ref[3 * leaves + begin:3 * leaves + end, :] * lax.rsqrt(jnp.full((1, LEAF), 0.01, F32))
    near_ref[...] = (near_ref[...] - times[begin:end] * itself) * (ULIST * LEAF) ** (-0.5)


GROUP = 16
SPREAD = 4


def down_kernel(
    counts_ref, gy_ref, counts_row_ref, nodes_ref, got_ref, vs_ref, vo_ref, near_ref, m2l_hbm, basis_hbm,
    pot_ref, m2l, basis, table, source, offset, tally, summed, local, far, sems,
):
    leaves = counts_row_ref.shape[1]
    m2l_copy = pltpu.make_async_copy(m2l_hbm, m2l, sems.at[0])
    basis_copy = pltpu.make_async_copy(basis_hbm, basis, sems.at[1])
    m2l_copy.start()
    basis_copy.start()
    gy = gy_ref[0]
    own = nodes_ref.shape[0]
    table[0:own, :] = nodes_ref[...]
    for s in range(SHIFTS):
        by = s + 1 if s < REACH else REACH - 1 - s
        block = 2 * ((gy - by) & (SHIFTS - 1)) + (0 if by > 0 else 1)
        table[own + s * CAP:own + (s + 1) * CAP, :] = got_ref[pl.ds(pl.multiple_of(block * CAP, CAP), CAP), :]
    top = own + SHIFTS * CAP
    table[top:, :] = jnp.zeros((table.shape[0] - top, MP), BF)
    offset[...] = jnp.full_like(offset, -1)
    offset[:, 0:VLIST] = vo_ref[...].astype(F32).T
    tally[...] = jnp.zeros_like(tally)
    source[...] = jnp.full_like(source, -1)
    source[:, 0:VLIST] = vs_ref[...].astype(F32).T
    sub = lax.broadcasted_iota(jnp.int32, (MP, MP), 0).astype(F32).astype(BF)
    one, zero = jnp.ones((), BF), jnp.zeros((), BF)
    F8 = jnp.float8_e4m3fn

    def group(g, _):
        for k in range(GROUP):
            l = g * GROUP + k
            o_row = offset[pl.ds(l, 1), :].astype(BF)
            o_hot = jnp.where(sub[0:OFFSETS] == o_row, one, zero).astype(F8)
            s_row = source[pl.ds(l, 1), :]
            for t in range(3):
                size = MP if t < 2 else 160
                part = jnp.clip(s_row - t * MP, -1.0, MP + 0.0).astype(BF)
                s_hot = jnp.where(sub[0:size] == part, one, zero).astype(F8)
                tally[k * OFFSETS:(k + 1) * OFFSETS, t * MP:t * MP + size] = lax.dot_general(
                    o_hot, s_hot, NT, preferred_element_type=F32
                ).astype(BF)
        both = dot(tally[...], table[...]).reshape(GROUP, OFFSETS, MP)
        summed[:, pl.ds(pl.multiple_of(g * GROUP, GROUP), GROUP), :] = jnp.swapaxes(both, 0, 1).astype(BF)
        return 0

    lax.fori_loop(0, leaves // GROUP, group, 0)
    m2l_copy.wait()
    local[...] = jnp.zeros_like(local)

    def translate(i, _):
        parts = [summed[i * 16 + k] for k in range(16)]
        local[...] += dot(jnp.concatenate(parts, axis=1), m2l[pl.ds(pl.multiple_of(i * 16 * MP, 16 * MP), 16 * MP), :])
        return 0

    lax.fori_loop(0, OFFSETS // 16, translate, 0)
    hi = local[...].astype(BF)
    lo = (local[...] - hi.astype(F32)).astype(BF)
    both = jnp.concatenate([hi, lo], axis=0)
    first, last = row_ranges(counts_row_ref[...])
    used = lax.fori_loop(0, leaves, lambda l, off: off + dense_rows(counts_ref[l]), jnp.int32(0))
    lane = lax.broadcasted_iota(jnp.int32, (leaves, ROWS), 1)
    basis_copy.wait()

    def expand(i, _):
        for part in range(SPREAD):
            j = i * SPREAD + part
            base = pl.multiple_of(j * ROWS, ROWS)
            p = lax.dot_general(both, basis[pl.ds(base, ROWS), :], NT, preferred_element_type=F32)
            p = p[:leaves] + p[leaves:]
            member = (lane >= first - base) & (lane < last - base)
            value = jnp.sum(jnp.where(member, p, 0.0), axis=0, keepdims=True)
            far[pl.ds(2 * j, 1), :] = value[:, :LEAF]
            far[pl.ds(2 * j + 1, 1), :] = value[:, LEAF:]
        return 0

    lax.fori_loop(0, (used + SPREAD * ROWS - 1) // (SPREAD * ROWS), expand, 0)
    lane1 = lax.broadcasted_iota(jnp.int32, (1, LEAF), 1)

    def place(i, off):
        parts = []
        for k in range(16):
            l = i * 16 + k
            row, at = off >> 7, off & (LEAF - 1)
            shift = (LEAF - at) & (LEAF - 1)
            a = pltpu.roll(far[pl.ds(row, 1), :], shift, 1)
            b = pltpu.roll(far[pl.ds(row + 1, 1), :], shift, 1)
            parts.append(jnp.where(lane1 < LEAF - at, a, b))
            off = off + dense_rows(counts_ref[l])
        pot_ref[pl.ds(pl.multiple_of(i * 16, 16), 16), :] = jnp.concatenate(parts, axis=0)
        return off

    lax.fori_loop(0, leaves // 16, place, jnp.int32(0))
    lane = lax.broadcasted_iota(jnp.int32, (leaves, LEAF), 1)
    value = pot_ref[...] * MP ** (-0.5) + near_ref[...]
    pot_ref[...] = jnp.where(lane < column(counts_row_ref[...]), value, 0.0)


def per_device(
    positions, charges, counts, centres, freqs, phases, m2m, m2l, send_nodes, v_source, v_offset, u_source
):
    leaves = counts.shape[0]
    n_gx, n_gy = lax.axis_size("gx"), lax.axis_size("gy")
    devices = n_gx * n_gy
    gy = lax.axis_index("gy").astype(jnp.int32).reshape(1)
    live = jnp.arange(LEAF, dtype=jnp.int32)[None, :] < counts[:, None]
    charge = jnp.where(live, charges.reshape(leaves, LEAF), 0.0)
    stacked = jnp.concatenate([positions.reshape(3 * leaves, LEAF), charge], axis=0)
    def swapped(first):
        lower = range(first, devices - 1, 2)
        return lax.ppermute(stacked, AXES, [(i, i + 1) for i in lower] + [(i + 1, i) for i in lower])

    evens, odds = swapped(0), swapped(1)
    odd = gy & 1

    counts_row = counts.reshape(1, leaves)
    dense_max = leaves * LEAF
    nodes_dev = leaves + leaves // 8
    limit = pltpu.CompilerParams(vmem_limit_bytes=60 * MIB)
    shape = jax.ShapeDtypeStruct
    vectors = (stacked, counts_row, freqs, phases.reshape(1, MP), send_nodes.reshape(SHIFTS, CAP))
    made = (
        shape((dense_max, MP), BF),
        shape((nodes_dev, MP), BF),
        shape((2 * SHIFTS * CAP, MP), BF),
        shape((REACH * CAP, MP), BF),
    )
    basis, nodes, slots, sel = pl.pallas_call(
        up_kernel,
        grid=(1,),
        out_shape=made,
        in_specs=[SM, SM, SM] + [block(v) for v in vectors] + [HBM],
        out_specs=[HBM] + [block(v) for v in made[1:]],
        scratch_shapes=[
            pltpu.VMEM((dense_max + STEP + LEAF, 32), F32),
            pltpu.VMEM((leaves, MP), F32),
            pltpu.VMEM((2, leaves, LEAF), F32),
            pltpu.VMEM((2, STEP, MP), BF),
            pltpu.VMEM(m2m.shape, BF),
            pltpu.VMEM((SHIFTS * CAP, MP), BF),
            pltpu.SemaphoreType.DMA((3,)),
        ],
        compiler_params=limit,
        cost_estimate=pl.CostEstimate(flops=10**9, bytes_accessed=10**7, transcendentals=4 * 10**6),
        name="upward",
    )(counts, centres.reshape(3 * leaves), gy, *vectors, m2m)

    across = []
    for i in range(devices):
        x, y = i // n_gy, i % n_gy
        to = x + 1 if y >= n_gy // 2 else x - 1
        if 0 <= to < n_gx:
            across.append((i, to * n_gy + y))
    recv = lax.ppermute(sel, AXES, across)

    nearby = (evens, stacked, odds, u_source.T)

    def near_part(begin, end, cost):
        return pl.pallas_call(
            functools.partial(near_kernel, begin, end),
            grid=(1,),
            out_shape=shape((end - begin, LEAF), F32),
            in_specs=[SM, SM, SM] + [block(v) for v in nearby],
            out_specs=pl.BlockSpec((end - begin, LEAF), lambda i: (0, 0)),
            scratch_shapes=[
                pltpu.VMEM((3 * leaves, 16, LEAF), BF),
                pltpu.VMEM((3 * leaves, 8, LEAF), F32),
                pltpu.VMEM((leaves * LEAF, 48), BF),
                pltpu.VMEM((leaves * LEAF + NEAR_BIG, LEAF), F32),
                pltpu.SMEM((2 * leaves + 16,), jnp.int32),
                pltpu.SMEM((2 * leaves + 16,), jnp.int32),
            ],
            compiler_params=limit,
            cost_estimate=pl.CostEstimate(flops=cost * 10**9, bytes_accessed=10**6, transcendentals=cost * 10**7),
            name="near",
        )(counts, odd, u_source.T.reshape(leaves * ULIST), *nearby)

    low = (gy[0] < n_gy // 2).astype(jnp.int32)
    slots = lax.dynamic_update_slice(
        slots.reshape(n_gy, 2, CAP, MP), recv.reshape(n_gy // 2, 1, CAP, MP), (low * (n_gy // 2), low, 0, 0)
    )
    got = lax.all_to_all(slots.reshape(n_gy, 2 * CAP, MP), "gy", 0, 0).reshape(2 * SHIFTS * CAP, MP)
    near_all = near_part(0, leaves, 8)

    table_rows = 3 * MP
    vectors = (counts_row, nodes, got, v_source.T, v_offset.T, near_all)
    out = pl.pallas_call(
        down_kernel,
        grid=(1,),
        out_shape=shape((leaves, LEAF), F32),
        in_specs=[SM, SM] + [block(v) for v in vectors] + [HBM, HBM],
        out_specs=block(charge),
        scratch_shapes=[
            pltpu.VMEM((OFFSETS * MP, MP), BF),
            pltpu.VMEM((dense_max, MP), BF),
            pltpu.VMEM((table_rows, MP), BF),
            pltpu.VMEM((leaves, MP), F32),
            pltpu.VMEM((leaves, MP), F32),
            pltpu.VMEM((GROUP * OFFSETS, table_rows), BF),
            pltpu.VMEM((OFFSETS, leaves, MP), BF),
            pltpu.VMEM((leaves, MP), F32),
            pltpu.VMEM((dense_max // LEAF + 8, LEAF), F32),
            pltpu.SemaphoreType.DMA((2,)),
        ],
        compiler_params=limit,
        cost_estimate=pl.CostEstimate(flops=2 * 10**10, bytes_accessed=2 * 10**7, transcendentals=0),
        name="downward",
    )(counts, gy, *vectors, m2l.reshape(OFFSETS * MP, MP), basis)
    return out.reshape(leaves * LEAF)


def solution(mesh):
    both = P(AXES)
    cols = P(None, AXES)
    in_specs = (
        cols, both, both, cols, P(), P(), P(), P(), P(AXES, None, None), P(AXES, None), P(AXES, None), P(AXES, None),
    )
    return jax.shard_map(per_device, mesh=mesh, in_specs=in_specs, out_specs=both, check_vma=False)
```
